32 devices in a mesh: gx: 8 (over z, y), gy: 4 (over x, core).
Axes of the slice: x: 2, y: 2, z: 4, core: 2. Of those that a mesh axis runs over, the one named last changes fastest.
Arguments:
- psi: float32 [64, 64, 1024], P(None, 'gx', 'gy'), may hold values from -500 to 500
- potential: float32 [64, 1024], P('gx', 'gy'), may hold values from -2 to 0
Outputs:
- orbitals: float32 [64, 64, 1024], P(None, 'gx', 'gy')
The draws below stay inside these ranges and needn't reach their ends.
All inputs are finite; a program needn't handle non-finite values.
Results may differ from the reference program's by a relative error of at most 0.0003.
Values sent between devices are 32-bit elements; how exact they have to be, the bound alone decides.
A program may use at most 64 MiB of HBM per device.

```python
import math
import jax
import jax.numpy as jnp
from jax import lax

M = 64
NZ = 64
NX = 64
NY = 16


def draw_psi(key, part):
    key_base = jax.random.fold_in(key, 11)
    key_scale = jax.random.fold_in(key, 12)
    key_shared = jax.random.fold_in(key, 13)
    key_offset = jax.random.fold_in(key, 14)
    key_mixing = jax.random.fold_in(key, 15)
    x_ramp = (3.0 ** (jnp.arange(NX, dtype=jnp.float32) / max(NX - 1, 1))).reshape(1, NX, 1)
    offset = jax.random.randint(key_offset, (), 0, M)
    rank_level = ((jnp.arange(M, dtype=jnp.int32) + offset) % M).astype(jnp.float32)
    own_weight = jnp.exp(-rank_level / max(M - 1, 1) * math.log(100.0)).reshape(M, 1, 1)
    shared_weight = jax.random.uniform(key_mixing, (M, 1, 1), jnp.float32, 0.5, 1.5)
    shared = jnp.clip(jax.random.normal(key_shared, (1, NX, NY * NZ), jnp.float32), -6.0, 6.0)
    independent = jnp.clip(jax.random.normal(key_base, (M, NX, NY * NZ), jnp.float32), -6.0, 6.0)
    cell_scale = jnp.exp(jax.random.uniform(key_scale, (1, NX, NY * NZ), jnp.float32) * math.log(10.0))
    values = (shared_weight * shared + own_weight * independent) * cell_scale * x_ramp
    return values.astype(jnp.float32)


def block_levels(key, dims, shards, low, high):
    loudness = 1.0
    for dim, parts in shards:
        steps = jax.random.uniform(jax.random.fold_in(jax.random.fold_in(key, 6), dim), (parts,), jnp.float32, low / len(shards), high / len(shards))
        loudness = loudness * jnp.repeat(jnp.exp(steps), dims[dim] // parts).reshape((-1,) + (1,) * (len(dims) - 1 - dim))
    return loudness


def setup_inputs(seed: int = 0) -> dict:
    key_list = jax.random.split(jax.random.key(seed), 3)
    psi = draw_psi(jax.random.fold_in(key_list[2], 71), 0)
    potential = jnp.clip(-2.0 + 2.0 * jax.random.uniform(key_list[1], (NX, NY * NZ), jnp.float32) ** block_levels(key_list[1], (NX, NY * NZ), ((0, 8), (1, 4)), -0.2, 0.2), -2.0, 0.0)
    return dict(psi=psi, potential=potential)


COEFS = (-205.0 / 72.0, 8.0 / 5.0, -1.0 / 5.0, 8.0 / 315.0, -1.0 / 560.0)
CENTER = 6.5
HALF_WIDTH = 5.5

def hamiltonian(orbital, field_pot):
    laplace = 3.0 * COEFS[0] * orbital
    for distance in range(1, 5):
        for axis_num in range(3):
            laplace = laplace + COEFS[distance] * (jnp.roll(orbital, distance, axis_num) + jnp.roll(orbital, -distance, axis_num))
    return -0.5 * laplace + field_pot * orbital

def orthonormal(matrix, ncount):
    gram_matrix = jnp.dot(matrix, matrix.T, precision=lax.Precision.HIGHEST) / ncount
    lower_factor = jnp.linalg.cholesky(gram_matrix)
    return lax.linalg.triangular_solve(lower_factor, matrix, left_side=True, lower=True)

def reference(psi, potential):
    field_pot = potential.reshape(NX, NY, NZ)

    def filter_one(orbital):
        initial = orbital.reshape(NX, NY, NZ)
        level_one = (hamiltonian(initial, field_pot) - CENTER * initial) / HALF_WIDTH
        second = 2.0 * (hamiltonian(level_one, field_pot) - CENTER * level_one) / HALF_WIDTH - initial
        filtered = 2.0 * (hamiltonian(second, field_pot) - CENTER * second) / HALF_WIDTH - level_one
        return filtered.reshape(NX, NY * NZ)
    filtered = lax.map(filter_one, psi)
    matrix = filtered.reshape(M, NX * NY * NZ)
    ncount = float(NX * NY * NZ)
    first_pass = orthonormal(matrix, ncount)
    final_pass = orthonormal(first_pass, ncount)
    return final_pass.reshape(M, NX, NY * NZ)
```

```python
import functools

import jax
import jax.numpy as jnp
from jax import lax
from jax.experimental import pallas as pl
from jax.experimental.pallas import tpu as pltpu
from jax.sharding import PartitionSpec as P

NZ = 64


COEFS = (-205.0 / 72.0, 8.0 / 5.0, -1.0 / 5.0, 8.0 / 315.0, -1.0 / 560.0)
CENTER = 6.5
HALF_WIDTH = 5.5


def padded(array, sides, width):
    for axis, dim in sides:
        size, length = (lax.axis_size(axis), array.shape[dim])
        up = [(i, (i + 1) % size) for i in range(size)]
        down = [(j, i) for i, j in up]
        last = lax.slice_in_dim(array, length - width, length, axis=dim)
        first = lax.slice_in_dim(array, 0, width, axis=dim)
        before = lax.ppermute(last, axis, up)
        after = lax.ppermute(first, axis, down)
        array = jnp.concatenate([before, array, after], axis=dim)
    return array


def along_third(field, depth_index):
    laplace = 3.0 * COEFS[0] * field
    for distance in range(1, 5):
        forward = jnp.where(
            depth_index < NZ - distance,
            jnp.roll(field, -distance, 2),
            jnp.roll(field, NZ - distance, 2),
        )
        behind = jnp.where(
            depth_index >= distance, jnp.roll(field, distance, 2), jnp.roll(field, distance - NZ, 2)
        )
        laplace = laplace + COEFS[distance] * (forward + behind)
    return laplace


def hamiltonian(field, field_pot, depth_index):
    row_count = field.shape[1]
    lane_count = field.shape[2]
    padded_x = padded(field, (("gx", 1),), 4)
    laplace = along_third(field, depth_index)
    padded_y = padded(field, (("gy", 2),), 4 * NZ)
    for distance in range(1, 5):
        laplace = laplace + COEFS[distance] * (
            padded_x[:, 4 + distance : 4 + distance + row_count]
            + padded_x[:, 4 - distance : 4 - distance + row_count]
        )
        ahead_start = (4 + distance) * NZ
        back_start = (4 - distance) * NZ
        laplace = laplace + COEFS[distance] * (
            padded_y[:, :, ahead_start : ahead_start + lane_count]
            + padded_y[:, :, back_start : back_start + lane_count]
        )
    return -0.5 * laplace + field_pot * field


def orthonormal(matrix, ncount):
    local_gram = jnp.dot(matrix, matrix.T, precision=lax.Precision.HIGHEST) / ncount
    total_gram = lax.psum(local_gram, ("gx", "gy"))
    lower_factor = jnp.linalg.cholesky(total_gram)
    return lax.linalg.triangular_solve(lower_factor, matrix, left_side=True, lower=True)


def on_device(psi, potential):
    orbit_count = psi.shape[0]
    row_count = psi.shape[1]
    lane_count = psi.shape[2]
    field_pot = potential.reshape(1, row_count, lane_count)
    depth_index = lax.broadcasted_iota(jnp.int32, (1, 1, lane_count), 2) % NZ
    level_one = (hamiltonian(psi, field_pot, depth_index) - CENTER * psi) / HALF_WIDTH
    second = (
        2.0 * (hamiltonian(level_one, field_pot, depth_index) - CENTER * level_one) / HALF_WIDTH
        - psi
    )
    filtered = (
        2.0 * (hamiltonian(second, field_pot, depth_index) - CENTER * second) / HALF_WIDTH
        - level_one
    )
    matrix = filtered.reshape(orbit_count, row_count * lane_count)
    ncount = float(row_count * lane_count * lax.axis_size("gx") * lax.axis_size("gy"))
    first_pass = orthonormal(matrix, ncount)
    final_pass = orthonormal(first_pass, ncount)
    return final_pass.reshape(orbit_count, row_count, lane_count)


MESH = pl.DeviceIdType.MESH
EXACT = lax.Precision.HIGHEST
LANES = 128


def z_matrix():
    row = lax.broadcasted_iota(jnp.int32, (LANES, LANES), 0)
    col = lax.broadcasted_iota(jnp.int32, (LANES, LANES), 1)
    same = (row // NZ) == (col // NZ)
    gap = (row - col + 2 * NZ) % NZ
    gap = jnp.minimum(gap, NZ - gap)
    matrix = jnp.zeros((LANES, LANES), jnp.float32)
    for distance in range(5):
        if distance == 0:
            value = (-1.5 * COEFS[0] - CENTER) / HALF_WIDTH
        else:
            value = -0.5 * COEFS[distance] / HALF_WIDTH
        matrix = jnp.where(same & (gap == distance), value, matrix)
    return matrix


def dot_nn(a, b):
    return lax.dot_general(a, b, (((1,), (0,)), ((), ())), precision=EXACT, preferred_element_type=jnp.float32)


def dot_nt(a, b):
    return lax.dot_general(a, b, (((1,), (1,)), ((), ())), precision=EXACT, preferred_element_type=jnp.float32)


def inverse_factor(gram):
    count = gram.shape[0]
    tiles = count // 8
    row_in = lax.broadcasted_iota(jnp.int32, (8, 2 * count), 0)
    lane = lax.broadcasted_iota(jnp.int32, (8, 2 * count), 1)
    blocks = []
    for i in range(tiles):
        eye = jnp.where(lane[:, :count] == row_in[:, :count] + 8 * i, 1.0, 0.0)
        blocks.append(jnp.concatenate([gram[8 * i : 8 * i + 8], eye], axis=1))
    for k in range(count - 1):
        tile, sub = k // 8, k % 8
        pivot_row = jnp.broadcast_to(blocks[tile][sub : sub + 1, :], (8, 2 * count))
        pivot = jnp.broadcast_to(pivot_row[:, k : k + 1], (8, 2 * count))
        scaled = pivot_row / pivot
        for i in range(tile, tiles):
            col = jnp.broadcast_to(blocks[i][:, k : k + 1], (8, 2 * count))
            if i == tile:
                col = jnp.where(row_in > sub, col, 0.0)
            blocks[i] = blocks[i] - col * scaled
    out = []
    for i in range(tiles):
        diagonal = jnp.sum(jnp.where(lane == row_in + 8 * i, blocks[i], 0.0), axis=1, keepdims=True)
        out.append(blocks[i][:, count:] / jnp.sqrt(diagonal))
    return jnp.concatenate(out, axis=0)


def kernel(
    nx, ny, psi_ref, pot_ref, out_ref,
    send, field, pots, work, half, zpart, back, block, matrix, part, sum_a, sum_b,
    psi_send, psi_recv, ret_send, ret_recv, pot_send, pot_recv, sum_send, sum_recv,
):
    devices = nx * ny
    orbits = psi_ref.shape[0]
    own = orbits // devices
    planes = devices // 8
    me = lax.axis_index("gx") * ny + lax.axis_index("gy")
    my_plane, my_place = me // 8, me % 8

    def device(target):
        return (target // ny, target % ny)

    def place_peer(step):
        return my_plane * 8 + lax.rem(my_place + step, 8)

    def plane_peer(step):
        return lax.rem(my_plane + step, planes) * 8 + my_place

    barrier = pltpu.get_barrier_semaphore()

    def greet(i, _):
        pl.semaphore_signal(barrier, inc=1, device_id=device(lax.rem(me + i, devices)), device_id_type=MESH)
        return 0

    lax.fori_loop(1, devices, greet, 0)

    for h in range(2):
        pots[my_place, my_plane, pl.ds(8 * h, 8), :] = pot_ref[:, h * LANES : (h + 1) * LANES] * (1.0 / HALF_WIDTH)
    for m in range(orbits):
        for h in range(2):
            send[16 * m + 8 * h : 16 * m + 8 * h + 8, :] = psi_ref[m, :, h * LANES : (h + 1) * LANES]

    pl.semaphore_wait(barrier, devices - 1)

    def copy_out(src, dst, sems, target):
        return pltpu.make_async_remote_copy(
            src_ref=src, dst_ref=dst, send_sem=sems[0], recv_sem=sems[1],
            device_id=device(target), device_id_type=MESH,
        )

    def drain(ref, sem):
        pltpu.make_async_copy(ref, ref, sem).wait()

    for step in range(1, planes):
        here = pots.at[my_place, my_plane]
        copy_out(here, here, (pot_send.at[0], pot_recv.at[0]), plane_peer(step)).start()

    def send_psi(o):
        def body(i, _):
            target = lax.rem(me + i + devices // 2, devices)

            @pl.when(target != me)
            def _():
                copy_out(
                    send.at[pl.ds((target * own + o) * 16, 16)], field.at[o, me],
                    (psi_send.at[o], psi_recv.at[o]), target,
                ).start()
            return 0

        lax.fori_loop(0, devices, body, 0)
        field[o, me] = send[pl.ds((me * own + o) * 16, 16), :]

    send_psi(0)
    drain(pots.at[0, pl.ds(0, planes - 1)], pot_recv.at[0])
    drain(pots.at[0, pl.ds(0, planes - 1)], pot_send.at[0])
    for step in range(1, 8):
        here = pots.at[my_place]
        copy_out(here, here, (pot_send.at[1], pot_recv.at[1]), place_peer(step)).start()
    for o in range(1, own):
        send_psi(o)

    zmat = z_matrix()
    tiles = 2 * ny
    rows = 8 * nx
    low = lax.broadcasted_iota(jnp.int32, (rows, LANES), 1) < NZ
    weights = [-0.5 * c / HALF_WIDTH for c in COEFS]

    def tile_of(ref, o, t):
        return jnp.concatenate(
            [ref[o, b * ny + t // 2, 8 * (t % 2) : 8 * (t % 2) + 8, :] for b in range(nx)], axis=0
        )

    def pot_tile(t):
        parts = []
        for b in range(nx):
            d = b * ny + t // 2
            parts.append(pots[d % 8, d // 8, 8 * (t % 2) : 8 * (t % 2) + 8, :])
        return jnp.concatenate(parts, axis=0)

    def apply(src, emit):
        zpart[...] = dot_nn(work[src].reshape(tiles * rows, LANES), zmat).reshape(tiles, rows, LANES)
        for t in range(tiles):
            half[t] = pltpu.roll(work[src, t], NZ, 1)
        for t in range(tiles):
            v = work[src, t]
            total = zpart[t] + pot_tile(t) * v
            for d in range(1, 5):
                total = total + weights[d] * (pltpu.roll(v, d, 0) + pltpu.roll(v, rows - d, 0))
            total = total + weights[2] * (work[src, (t + 1) % tiles] + work[src, (t - 1) % tiles])
            total = total + weights[4] * (work[src, (t + 2) % tiles] + work[src, (t - 2) % tiles])
            s = [half[(t + k) % tiles] for k in range(-2, 3)]
            total = total + weights[1] * (s[2] + jnp.where(low, s[1], s[3]))
            total = total + weights[3] * jnp.where(low, s[3] + s[0], s[4] + s[1])
            emit(t, total)

    def send_back(o):
        def body(i, _):
            target = lax.rem(me + i + devices // 2, devices)

            @pl.when(target != me)
            def _():
                copy_out(
                    back.at[o, target], block.at[pl.ds((me * own + o) * 16, 16)],
                    (ret_send.at[o], ret_recv), target,
                ).start()
            return 0

        lax.fori_loop(0, devices, body, 0)
        block[pl.ds((me * own + o) * 16, 16), :] = back[o, me]

    for o in range(own):
        drain(field.at[o, pl.ds(0, devices - 1)], psi_recv.at[o])
        if o == 0:
            drain(pots.at[pl.ds(0, 7)], pot_recv.at[1])
        for t in range(tiles):
            work[0, t] = tile_of(field, o, t)

        def emit_one(t, value):
            work[1, t] = value

        def emit_two(t, value):
            work[2, t] = 2.0 * value - work[0, t]

        def emit_three(t, value):
            value = 2.0 * value - work[1, t]
            for b in range(nx):
                back[o, b * ny + t // 2, 8 * (t % 2) : 8 * (t % 2) + 8, :] = value[8 * b : 8 * b + 8]

        apply(0, emit_one)
        apply(1, emit_two)
        apply(2, emit_three)
        send_back(o)

    drain(pots.at[pl.ds(0, 7)], pot_send.at[1])
    for o in range(own):
        drain(field.at[o, pl.ds(0, devices - 1)], psi_send.at[o])
        drain(back.at[o, pl.ds(0, devices - 1)], ret_send.at[o])
    drain(block.at[pl.ds(0, (devices - 1) * own * 16)], ret_recv)

    for j in range(16):
        matrix[:, j * LANES : (j + 1) * LANES] = block[pl.ds(j, orbits, stride=16), :]

    ncount = float(rows * tiles * LANES)
    halfrows = orbits // 2

    def total_gram(turn, local):
        local = jnp.concatenate([local[:halfrows], local[halfrows:]], axis=1)
        sum_a[turn, my_plane] = local
        for step in range(1, planes):
            here = sum_a.at[turn, my_plane]
            copy_out(here, here, (sum_send.at[turn, 0], sum_recv.at[turn, 0]), plane_peer(step)).start()
        drain(sum_a.at[turn, pl.ds(0, planes - 1)], sum_recv.at[turn, 0])
        drain(sum_a.at[turn, pl.ds(0, planes - 1)], sum_send.at[turn, 0])
        total = sum_a[turn, 0]
        for i in range(1, planes):
            total = total + sum_a[turn, i]
        sum_b[turn, my_place] = total
        for step in range(1, 8):
            here = sum_b.at[turn, my_place]
            copy_out(here, here, (sum_send.at[turn, 1], sum_recv.at[turn, 1]), place_peer(step)).start()
        drain(sum_b.at[turn, pl.ds(0, 7)], sum_recv.at[turn, 1])
        drain(sum_b.at[turn, pl.ds(0, 7)], sum_send.at[turn, 1])
        total = sum_b[turn, 0]
        for i in range(1, 8):
            total = total + sum_b[turn, i]
        total = total * (1.0 / ncount)
        return jnp.concatenate([total[:, :orbits], total[:, orbits:]], axis=0)

    for turn in range(2):
        x = matrix[...]
        gram = total_gram(turn, dot_nt(x, x))
        matrix[...] = dot_nn(inverse_factor(gram), matrix[...])
    for j in range(16):
        block[pl.ds(j, orbits, stride=16), :] = matrix[:, j * LANES : (j + 1) * LANES]
    for m in range(orbits):
        for h in range(2):
            out_ref[m, :, h * LANES : (h + 1) * LANES] = block[16 * m + 8 * h : 16 * m + 8 * h + 8, :]


def transposed(nx, ny, psi, potential):
    orbits = psi.shape[0]
    devices = nx * ny
    own = orbits // devices
    f32 = jnp.float32
    tiles, rows = 2 * ny, 8 * nx
    dma = pltpu.SemaphoreType.DMA
    return pl.pallas_call(
        functools.partial(kernel, nx, ny),
        out_shape=jax.ShapeDtypeStruct(psi.shape, f32),
        in_specs=[pl.BlockSpec(memory_space=pltpu.VMEM)] * 2,
        out_specs=pl.BlockSpec(memory_space=pltpu.VMEM),
        scratch_shapes=[
            pltpu.VMEM((orbits * 16, LANES), f32),
            pltpu.VMEM((own, devices, 16, LANES), f32),
            pltpu.VMEM((8, devices // 8, 16, LANES), f32),
            pltpu.VMEM((3, tiles, rows, LANES), f32),
            pltpu.VMEM((tiles, rows, LANES), f32),
            pltpu.VMEM((tiles, rows, LANES), f32),
            pltpu.VMEM((own, devices, 16, LANES), f32),
            pltpu.VMEM((orbits * 16, LANES), f32),
            pltpu.VMEM((orbits, 16 * LANES), f32),
            pltpu.VMEM((8, LANES), f32),
            pltpu.VMEM((2, devices // 8, orbits // 2, 2 * orbits), f32),
            pltpu.VMEM((2, 8, orbits // 2, 2 * orbits), f32),
            dma((own,)), dma((own,)), dma((own,)), dma,
            dma((2,)), dma((2,)), dma((2, 2)), dma((2, 2)),
        ],
        compiler_params=pltpu.CompilerParams(
            collective_id=0, has_side_effects=True, vmem_limit_bytes=48 * 1024 * 1024
        ),
    )(psi, potential)


def solution(mesh):
    in_specs = (P(None, "gx", "gy"), P("gx", "gy"))
    out_specs = P(None, "gx", "gy")
    nx, ny = mesh.shape["gx"], mesh.shape["gy"]

    def step(psi, potential):
        orbits, rows, lanes = psi.shape
        whole_orbits = orbits % (nx * ny) == 0 and (nx * ny) % 16 == 0
        if whole_orbits and rows == 8 and lanes == 2 * LANES and orbits == 64 and ny >= 4:
            return transposed(nx, ny, psi, potential)
        return on_device(psi, potential)

    return jax.shard_map(step, mesh=mesh, in_specs=in_specs, out_specs=out_specs, check_vma=False)
```

```python
import functools

import jax
import jax.numpy as jnp
from jax import lax
from jax.experimental import pallas as pl
from jax.experimental.pallas import tpu as pltpu
from jax.sharding import PartitionSpec as P

NZ = 64


COEFS = (-205.0 / 72.0, 8.0 / 5.0, -1.0 / 5.0, 8.0 / 315.0, -1.0 / 560.0)
CENTER = 6.5
HALF_WIDTH = 5.5


def padded(array, sides, width):
    for axis, dim in sides:
        size, length = (lax.axis_size(axis), array.shape[dim])
        up = [(i, (i + 1) % size) for i in range(size)]
        down = [(j, i) for i, j in up]
        last = lax.slice_in_dim(array, length - width, length, axis=dim)
        first = lax.slice_in_dim(array, 0, width, axis=dim)
        before = lax.ppermute(last, axis, up)
        after = lax.ppermute(first, axis, down)
        array = jnp.concatenate([before, array, after], axis=dim)
    return array


def along_third(field, depth_index):
    laplace = 3.0 * COEFS[0] * field
    for distance in range(1, 5):
        forward = jnp.where(
            depth_index < NZ - distance,
            jnp.roll(field, -distance, 2),
            jnp.roll(field, NZ - distance, 2),
        )
        behind = jnp.where(
            depth_index >= distance, jnp.roll(field, distance, 2), jnp.roll(field, distance - NZ, 2)
        )
        laplace = laplace + COEFS[distance] * (forward + behind)
    return laplace


def hamiltonian(field, field_pot, depth_index):
    row_count = field.shape[1]
    lane_count = field.shape[2]
    padded_x = padded(field, (("gx", 1),), 4)
    laplace = along_third(field, depth_index)
    padded_y = padded(field, (("gy", 2),), 4 * NZ)
    for distance in range(1, 5):
        laplace = laplace + COEFS[distance] * (
            padded_x[:, 4 + distance : 4 + distance + row_count]
            + padded_x[:, 4 - distance : 4 - distance + row_count]
        )
        ahead_start = (4 + distance) * NZ
        back_start = (4 - distance) * NZ
        laplace = laplace + COEFS[distance] * (
            padded_y[:, :, ahead_start : ahead_start + lane_count]
            + padded_y[:, :, back_start : back_start + lane_count]
        )
    return -0.5 * laplace + field_pot * field


def orthonormal(matrix, ncount):
    local_gram = jnp.dot(matrix, matrix.T, precision=lax.Precision.HIGHEST) / ncount
    total_gram = lax.psum(local_gram, ("gx", "gy"))
    lower_factor = jnp.linalg.cholesky(total_gram)
    return lax.linalg.triangular_solve(lower_factor, matrix, left_side=True, lower=True)


def on_device(psi, potential):
    orbit_count = psi.shape[0]
    row_count = psi.shape[1]
    lane_count = psi.shape[2]
    field_pot = potential.reshape(1, row_count, lane_count)
    depth_index = lax.broadcasted_iota(jnp.int32, (1, 1, lane_count), 2) % NZ
    level_one = (hamiltonian(psi, field_pot, depth_index) - CENTER * psi) / HALF_WIDTH
    second = (
        2.0 * (hamiltonian(level_one, field_pot, depth_index) - CENTER * level_one) / HALF_WIDTH
        - psi
    )
    filtered = (
        2.0 * (hamiltonian(second, field_pot, depth_index) - CENTER * second) / HALF_WIDTH
        - level_one
    )
    matrix = filtered.reshape(orbit_count, row_count * lane_count)
    ncount = float(row_count * lane_count * lax.axis_size("gx") * lax.axis_size("gy"))
    first_pass = orthonormal(matrix, ncount)
    final_pass = orthonormal(first_pass, ncount)
    return final_pass.reshape(orbit_count, row_count, lane_count)


MESH = pl.DeviceIdType.MESH
EXACT = lax.Precision.HIGHEST
LANES = 128


def z_matrix():
    row = lax.broadcasted_iota(jnp.int32, (LANES, LANES), 0)
    col = lax.broadcasted_iota(jnp.int32, (LANES, LANES), 1)
    same = (row // NZ) == (col // NZ)
    gap = (row - col + 2 * NZ) % NZ
    gap = jnp.minimum(gap, NZ - gap)
    matrix = jnp.zeros((LANES, LANES), jnp.float32)
    for distance in range(5):
        if distance == 0:
            value = (-1.5 * COEFS[0] - CENTER) / HALF_WIDTH
        else:
            value = -0.5 * COEFS[distance] / HALF_WIDTH
        matrix = jnp.where(same & (gap == distance), value, matrix)
    return matrix


def dot_nn(a, b):
    return lax.dot_general(a, b, (((1,), (0,)), ((), ())), precision=EXACT, preferred_element_type=jnp.float32)


def dot_nt(a, b):
    return lax.dot_general(a, b, (((1,), (1,)), ((), ())), precision=EXACT, preferred_element_type=jnp.float32)


def inverse_factor(gram):
    count = gram.shape[0]
    tiles = count // 8
    shape = (8, 2 * count)
    row_in = lax.broadcasted_iota(jnp.int32, shape, 0)
    lane = lax.broadcasted_iota(jnp.int32, shape, 1)
    blocks = []
    for i in range(tiles):
        eye = jnp.where(lane[:, :count] == row_in[:, :count] + 8 * i, 1.0, 0.0)
        blocks.append(jnp.concatenate([gram[8 * i : 8 * i + 8], eye], axis=1))

    def row_of(array, j):
        return jnp.broadcast_to(array[j : j + 1, :], shape)

    out = []
    for t in range(tiles):
        cols = [[jnp.broadcast_to(blocks[i][:, 8 * t + j : 8 * t + j + 1], shape) for j in range(8)] for i in range(t, tiles)]
        diag = [[row_of(cols[0][j], a) if a >= j else None for j in range(8)] for a in range(8)]
        inverse, pivots = [], []
        factor = [[None] * 8 for _ in range(8)]
        for j in range(8):
            pivots.append(diag[j][j])
            inverse.append(1.0 / diag[j][j])
            for a in range(j + 1, 8):
                factor[a][j] = diag[a][j] * inverse[j]
            for a in range(j + 1, 8):
                for b in range(j + 1, a + 1):
                    diag[a][b] = diag[a][b] - factor[a][j] * diag[b][j]
        current = blocks[t]
        finished = []
        for j in range(8):
            finished.append(row_of(current, j))
            if j < 7:
                below = jnp.zeros(shape, jnp.float32)
                for a in range(j + 1, 8):
                    below = jnp.where(row_in == a, factor[a][j], below)
                current = current - below * finished[j]
        blocks[t] = current
        for i in range(t + 1, tiles):
            col = cols[i - t]
            total = blocks[i]
            for j in range(8):
                scaled = col[j] * inverse[j]
                total = total - scaled * finished[j]
                for b in range(j + 1, 8):
                    col[b] = col[b] - scaled * diag[b][j]
            blocks[i] = total
        pivot = pivots[0]
        for j in range(1, 8):
            pivot = jnp.where(row_in == j, pivots[j], pivot)
        out.append((current / jnp.sqrt(pivot))[:, count:])
    return jnp.concatenate(out, axis=0)


def kernel(
    nx, ny, psi_ref, pot_ref, out_ref,
    send, field, pots, work, half, zpart, back, block, matrix, pot_in, sum_a, sum_b, load_sem,
    psi_send, psi_recv, ret_send, ret_recv, pot_send, pot_recv, sum_send, sum_recv,
):
    devices = nx * ny
    orbits = psi_ref.shape[0]
    own = orbits // devices
    planes = devices // 8
    me = lax.axis_index("gx") * ny + lax.axis_index("gy")
    my_plane, my_place = me // 8, me % 8

    def device(target):
        return (target // ny, target % ny)

    def place_peer(step):
        return my_plane * 8 + lax.rem(my_place + step, 8)

    def plane_peer(step):
        return lax.rem(my_plane + step, planes) * 8 + my_place

    loads = []
    for h in range(2):
        half_lanes = pl.ds(h * LANES, LANES)
        loads.append(pltpu.make_async_copy(
            psi_ref.at[:, :, half_lanes], send.at[:, pl.ds(8 * h, 8), :], load_sem.at[h]))
    for h in range(2):
        half_lanes = pl.ds(h * LANES, LANES)
        loads.append(pltpu.make_async_copy(
            pot_ref.at[:, half_lanes], pot_in.at[pl.ds(8 * h, 8), :], load_sem.at[2 + h]))
    for c in loads:
        c.start()

    barrier = pltpu.get_barrier_semaphore()

    def greet(i, _):
        pl.semaphore_signal(barrier, inc=1, device_id=device(lax.rem(me + i, devices)), device_id_type=MESH)
        return 0

    lax.fori_loop(1, devices, greet, 0)

    for c in loads[2:]:
        c.wait()
    pots[my_place, my_plane] = pot_in[...] * (1.0 / HALF_WIDTH)
    pl.semaphore_wait(barrier, devices - 1)

    def copy_out(src, dst, sems, target):
        return pltpu.make_async_remote_copy(
            src_ref=src, dst_ref=dst, send_sem=sems[0], recv_sem=sems[1],
            device_id=device(target), device_id_type=MESH,
        )

    def drain(ref, sem):
        pltpu.make_async_copy(ref, ref, sem).wait()

    for step in range(1, planes):
        here = pots.at[my_place, my_plane]
        copy_out(here, here, (pot_send.at[0], pot_recv.at[0]), plane_peer(step)).start()

    def send_psi(o):
        def body(i, _):
            target = lax.rem(me + i + devices // 2, devices)

            @pl.when(target != me)
            def _():
                copy_out(
                    send.at[target * own + o], field.at[o, me],
                    (psi_send.at[o], psi_recv.at[o]), target,
                ).start()
            return 0

        lax.fori_loop(0, devices, body, 0)
        field[o, me] = send[me * own + o]

    for c in loads[:2]:
        c.wait()
    send_psi(0)
    drain(pots.at[0, pl.ds(0, planes - 1)], pot_recv.at[0])
    drain(pots.at[0, pl.ds(0, planes - 1)], pot_send.at[0])
    for step in range(1, 8):
        here = pots.at[my_place]
        copy_out(here, here, (pot_send.at[1], pot_recv.at[1]), place_peer(step)).start()
    for o in range(1, own):
        send_psi(o)

    zmat = z_matrix()
    tiles = 2 * ny
    rows = 8 * nx
    low = lax.broadcasted_iota(jnp.int32, (rows, LANES), 1) < NZ
    weights = [-0.5 * c / HALF_WIDTH for c in COEFS]

    def tile_of(ref, o, t):
        return jnp.concatenate(
            [ref[o, b * ny + t // 2, 8 * (t % 2) : 8 * (t % 2) + 8, :] for b in range(nx)], axis=0
        )

    def pot_tile(t):
        parts = []
        for b in range(nx):
            d = b * ny + t // 2
            parts.append(pots[d % 8, d // 8, 8 * (t % 2) : 8 * (t % 2) + 8, :])
        return jnp.concatenate(parts, axis=0)

    def apply(src, emit):
        zpart[...] = dot_nn(work[src].reshape(tiles * rows, LANES), zmat).reshape(tiles, rows, LANES)
        for t in range(tiles):
            half[t] = pltpu.roll(work[src, t], NZ, 1)
        for t in range(tiles):
            v = work[src, t]
            total = zpart[t] + pot_tile(t) * v
            for d in range(1, 5):
                total = total + weights[d] * (pltpu.roll(v, d, 0) + pltpu.roll(v, rows - d, 0))
            total = total + weights[2] * (work[src, (t + 1) % tiles] + work[src, (t - 1) % tiles])
            total = total + weights[4] * (work[src, (t + 2) % tiles] + work[src, (t - 2) % tiles])
            s = [half[(t + k) % tiles] for k in range(-2, 3)]
            total = total + weights[1] * (s[2] + jnp.where(low, s[1], s[3]))
            total = total + weights[3] * jnp.where(low, s[3] + s[0], s[4] + s[1])
            emit(t, total)

    def send_back(o):
        def body(i, _):
            target = lax.rem(me + i + devices // 2, devices)

            @pl.when(target != me)
            def _():
                copy_out(
                    back.at[o, target], block.at[pl.ds((me * own + o) * 16, 16)],
                    (ret_send.at[o], ret_recv), target,
                ).start()
            return 0

        lax.fori_loop(0, devices, body, 0)
        block[pl.ds((me * own + o) * 16, 16), :] = back[o, me]

    for o in range(own):
        drain(field.at[o, pl.ds(0, devices - 1)], psi_recv.at[o])
        if o == 0:
            drain(pots.at[pl.ds(0, 7)], pot_recv.at[1])
        for t in range(tiles):
            work[0, t] = tile_of(field, o, t)

        def emit_one(t, value):
            work[1, t] = value

        def emit_two(t, value):
            work[2, t] = 2.0 * value - work[0, t]

        def emit_three(t, value):
            value = 2.0 * value - work[1, t]
            for b in range(nx):
                back[o, b * ny + t // 2, 8 * (t % 2) : 8 * (t % 2) + 8, :] = value[8 * b : 8 * b + 8]

        apply(0, emit_one)
        apply(1, emit_two)
        apply(2, emit_three)
        send_back(o)

    drain(pots.at[pl.ds(0, 7)], pot_send.at[1])
    for o in range(own):
        drain(field.at[o, pl.ds(0, devices - 1)], psi_send.at[o])
        drain(back.at[o, pl.ds(0, devices - 1)], ret_send.at[o])
    drain(block.at[pl.ds(0, (devices - 1) * own * 16)], ret_recv)

    for j in range(16):
        matrix[:, j * LANES : (j + 1) * LANES] = block[pl.ds(j, orbits, stride=16), :]

    ncount = float(rows * tiles * LANES)
    halfrows = orbits // 2

    def total_gram(turn, local):
        local = jnp.concatenate([local[:halfrows], local[halfrows:]], axis=1)
        sum_a[turn, my_plane] = local
        for step in range(1, planes):
            here = sum_a.at[turn, my_plane]
            copy_out(here, here, (sum_send.at[turn, 0], sum_recv.at[turn, 0]), plane_peer(step)).start()
        drain(sum_a.at[turn, pl.ds(0, planes - 1)], sum_recv.at[turn, 0])
        drain(sum_a.at[turn, pl.ds(0, planes - 1)], sum_send.at[turn, 0])
        total = sum_a[turn, 0]
        for i in range(1, planes):
            total = total + sum_a[turn, i]
        sum_b[turn, my_place] = total
        for step in range(1, 8):
            here = sum_b.at[turn, my_place]
            copy_out(here, here, (sum_send.at[turn, 1], sum_recv.at[turn, 1]), place_peer(step)).start()
        drain(sum_b.at[turn, pl.ds(0, 7)], sum_recv.at[turn, 1])
        drain(sum_b.at[turn, pl.ds(0, 7)], sum_send.at[turn, 1])
        total = sum_b[turn, 0]
        for i in range(1, 8):
            total = total + sum_b[turn, i]
        total = total * (1.0 / ncount)
        return jnp.concatenate([total[:, :orbits], total[:, orbits:]], axis=0)

    for turn in range(2):
        x = matrix[...]
        gram = total_gram(turn, dot_nt(x, x))
        matrix[...] = dot_nn(inverse_factor(gram), matrix[...])
    for j in range(16):
        block[pl.ds(j, orbits, stride=16), :] = matrix[:, j * LANES : (j + 1) * LANES]
    for m in range(orbits):
        for h in range(2):
            out_ref[m, :, h * LANES : (h + 1) * LANES] = block[16 * m + 8 * h : 16 * m + 8 * h + 8, :]


def transposed(nx, ny, psi, potential):
    orbits = psi.shape[0]
    devices = nx * ny
    own = orbits // devices
    f32 = jnp.float32
    tiles, rows = 2 * ny, 8 * nx
    dma = pltpu.SemaphoreType.DMA
    return pl.pallas_call(
        functools.partial(kernel, nx, ny),
        out_shape=jax.ShapeDtypeStruct(psi.shape, f32),
        in_specs=[pl.BlockSpec(memory_space=pl.ANY)] * 2,
        out_specs=pl.BlockSpec(memory_space=pltpu.VMEM),
        scratch_shapes=[
            pltpu.VMEM((orbits, 16, LANES), f32),
            pltpu.VMEM((own, devices, 16, LANES), f32),
            pltpu.VMEM((8, devices // 8, 16, LANES), f32),
            pltpu.VMEM((3, tiles, rows, LANES), f32),
            pltpu.VMEM((tiles, rows, LANES), f32),
            pltpu.VMEM((tiles, rows, LANES), f32),
            pltpu.VMEM((own, devices, 16, LANES), f32),
            pltpu.VMEM((orbits * 16, LANES), f32),
            pltpu.VMEM((orbits, 16 * LANES), f32),
            pltpu.VMEM((16, LANES), f32),
            pltpu.VMEM((2, devices // 8, orbits // 2, 2 * orbits), f32),
            pltpu.VMEM((2, 8, orbits // 2, 2 * orbits), f32),
            dma((4,)), dma((own,)), dma((own,)), dma((own,)), dma,
            dma((2,)), dma((2,)), dma((2, 2)), dma((2, 2)),
        ],
        compiler_params=pltpu.CompilerParams(
            collective_id=0, has_side_effects=True, vmem_limit_bytes=48 * 1024 * 1024
        ),
    )(psi, potential)


def solution(mesh):
    in_specs = (P(None, "gx", "gy"), P("gx", "gy"))
    out_specs = P(None, "gx", "gy")
    nx, ny = mesh.shape["gx"], mesh.shape["gy"]

    def step(psi, potential):
        orbits, rows, lanes = psi.shape
        whole_orbits = orbits % (nx * ny) == 0 and (nx * ny) % 16 == 0
        if whole_orbits and rows == 8 and lanes == 2 * LANES and orbits == 64 and ny >= 4:
            return transposed(nx, ny, psi, potential)
        return on_device(psi, potential)

    return jax.shard_map(step, mesh=mesh, in_specs=in_specs, out_specs=out_specs, check_vma=False)
```

```python
import functools
import math

import jax
import jax.numpy as jnp
from jax import lax
from jax.experimental import pallas as pl
from jax.experimental.pallas import tpu as pltpu
from jax.sharding import PartitionSpec as P

NZ = 64


COEFS = (-205.0 / 72.0, 8.0 / 5.0, -1.0 / 5.0, 8.0 / 315.0, -1.0 / 560.0)
CENTER = 6.5
HALF_WIDTH = 5.5


def padded(array, sides, width):
    for axis, dim in sides:
        size, length = (lax.axis_size(axis), array.shape[dim])
        up = [(i, (i + 1) % size) for i in range(size)]
        down = [(j, i) for i, j in up]
        last = lax.slice_in_dim(array, length - width, length, axis=dim)
        first = lax.slice_in_dim(array, 0, width, axis=dim)
        before = lax.ppermute(last, axis, up)
        after = lax.ppermute(first, axis, down)
        array = jnp.concatenate([before, array, after], axis=dim)
    return array


def along_third(field, depth_index):
    laplace = 3.0 * COEFS[0] * field
    for distance in range(1, 5):
        forward = jnp.where(
            depth_index < NZ - distance,
            jnp.roll(field, -distance, 2),
            jnp.roll(field, NZ - distance, 2),
        )
        behind = jnp.where(
            depth_index >= distance, jnp.roll(field, distance, 2), jnp.roll(field, distance - NZ, 2)
        )
        laplace = laplace + COEFS[distance] * (forward + behind)
    return laplace


def hamiltonian(field, field_pot, depth_index):
    row_count = field.shape[1]
    lane_count = field.shape[2]
    padded_x = padded(field, (("gx", 1),), 4)
    laplace = along_third(field, depth_index)
    padded_y = padded(field, (("gy", 2),), 4 * NZ)
    for distance in range(1, 5):
        laplace = laplace + COEFS[distance] * (
            padded_x[:, 4 + distance : 4 + distance + row_count]
            + padded_x[:, 4 - distance : 4 - distance + row_count]
        )
        ahead_start = (4 + distance) * NZ
        back_start = (4 - distance) * NZ
        laplace = laplace + COEFS[distance] * (
            padded_y[:, :, ahead_start : ahead_start + lane_count]
            + padded_y[:, :, back_start : back_start + lane_count]
        )
    return -0.5 * laplace + field_pot * field


def orthonormal(matrix, ncount):
    local_gram = jnp.dot(matrix, matrix.T, precision=lax.Precision.HIGHEST) / ncount
    total_gram = lax.psum(local_gram, ("gx", "gy"))
    lower_factor = jnp.linalg.cholesky(total_gram)
    return lax.linalg.triangular_solve(lower_factor, matrix, left_side=True, lower=True)


def on_device(psi, potential):
    orbit_count = psi.shape[0]
    row_count = psi.shape[1]
    lane_count = psi.shape[2]
    field_pot = potential.reshape(1, row_count, lane_count)
    depth_index = lax.broadcasted_iota(jnp.int32, (1, 1, lane_count), 2) % NZ
    level_one = (hamiltonian(psi, field_pot, depth_index) - CENTER * psi) / HALF_WIDTH
    second = (
        2.0 * (hamiltonian(level_one, field_pot, depth_index) - CENTER * level_one) / HALF_WIDTH
        - psi
    )
    filtered = (
        2.0 * (hamiltonian(second, field_pot, depth_index) - CENTER * second) / HALF_WIDTH
        - level_one
    )
    matrix = filtered.reshape(orbit_count, row_count * lane_count)
    ncount = float(row_count * lane_count * lax.axis_size("gx") * lax.axis_size("gy"))
    first_pass = orthonormal(matrix, ncount)
    final_pass = orthonormal(first_pass, ncount)
    return final_pass.reshape(orbit_count, row_count, lane_count)


MESH = pl.DeviceIdType.MESH
EXACT = lax.Precision.HIGHEST
LANES = 128


def z_matrix():
    row = lax.broadcasted_iota(jnp.int32, (LANES, LANES), 0)
    col = lax.broadcasted_iota(jnp.int32, (LANES, LANES), 1)
    same = (row // NZ) == (col // NZ)
    gap = (row - col + 2 * NZ) % NZ
    gap = jnp.minimum(gap, NZ - gap)
    matrix = jnp.zeros((LANES, LANES), jnp.float32)
    for distance in range(5):
        if distance == 0:
            value = (-1.5 * COEFS[0] - CENTER) / HALF_WIDTH
        else:
            value = -0.5 * COEFS[distance] / HALF_WIDTH
        matrix = jnp.where(same & (gap == distance), value, matrix)
    return matrix


def dot_nn(a, b):
    return lax.dot_general(a, b, (((1,), (0,)), ((), ())), precision=EXACT, preferred_element_type=jnp.float32)


def dot_nt(a, b):
    return lax.dot_general(a, b, (((1,), (1,)), ((), ())), precision=EXACT, preferred_element_type=jnp.float32)


def inverse_factor(gram):
    count = gram.shape[0]
    tiles = count // 8
    shape = (8, 2 * count)
    row_in = lax.broadcasted_iota(jnp.int32, shape, 0)
    lane = lax.broadcasted_iota(jnp.int32, shape, 1)
    blocks = []
    for i in range(tiles):
        eye = jnp.where(lane[:, :count] == row_in[:, :count] + 8 * i, 1.0, 0.0)
        blocks.append(jnp.concatenate([gram[8 * i : 8 * i + 8], eye], axis=1))

    def row_of(array, j):
        return jnp.broadcast_to(array[j : j + 1, :], shape)

    out = []
    for t in range(tiles):
        cols = [[jnp.broadcast_to(blocks[i][:, 8 * t + j : 8 * t + j + 1], shape) for j in range(8)] for i in range(t, tiles)]
        diag = [[row_of(cols[0][j], a) if a >= j else None for j in range(8)] for a in range(8)]
        inverse, pivots = [], []
        factor = [[None] * 8 for _ in range(8)]
        for j in range(8):
            pivots.append(diag[j][j])
            guess = pl.reciprocal(diag[j][j], approx=True)
            guess = guess * (2.0 - diag[j][j] * guess)
            inverse.append(guess * (2.0 - diag[j][j] * guess))
            for a in range(j + 1, 8):
                factor[a][j] = diag[a][j] * inverse[j]
            for a in range(j + 1, 8):
                for b in range(j + 1, a + 1):
                    diag[a][b] = diag[a][b] - factor[a][j] * diag[b][j]
        current = blocks[t]
        finished = []
        for j in range(8):
            finished.append(row_of(current, j))
            if j < 7:
                below = jnp.zeros(shape, jnp.float32)
                for a in range(j + 1, 8):
                    below = jnp.where(row_in == a, factor[a][j], below)
                current = current - below * finished[j]
        blocks[t] = current
        for i in range(t + 1, tiles):
            col = cols[i - t]
            total = blocks[i]
            for j in range(8):
                scaled = col[j] * inverse[j]
                total = total - scaled * finished[j]
                for b in range(j + 1, 8):
                    col[b] = col[b] - scaled * diag[b][j]
            blocks[i] = total
        pivot = pivots[0]
        for j in range(1, 8):
            pivot = jnp.where(row_in == j, pivots[j], pivot)
        out.append((current / jnp.sqrt(pivot))[:, count:])
    return jnp.concatenate(out, axis=0)


def kernel(
    nx, ny, psi_ref, pot_ref, out_ref,
    send, field, pots, work, half, zpart, back, block, matrix, pot_in, sum_a, sum_b, load_sem,
    psi_send, psi_recv, ret_send, ret_recv, pot_send, pot_recv, sum_send, sum_recv,
):
    devices = nx * ny
    orbits = psi_ref.shape[0]
    own = orbits // devices
    planes = devices // 8
    me = lax.axis_index("gx") * ny + lax.axis_index("gy")
    my_plane, my_place = me // 8, me % 8

    def device(target):
        return (target // ny, target % ny)

    def place_peer(step):
        return my_plane * 8 + lax.rem(my_place + step, 8)

    def plane_peer(step):
        return lax.rem(my_plane + step, planes) * 8 + my_place

    loads = []
    for h in range(2):
        half_lanes = pl.ds(h * LANES, LANES)
        loads.append(pltpu.make_async_copy(
            psi_ref.at[:, :, half_lanes], send.at[:, pl.ds(8 * h, 8), :], load_sem.at[h]))
    for h in range(2):
        half_lanes = pl.ds(h * LANES, LANES)
        loads.append(pltpu.make_async_copy(
            pot_ref.at[:, half_lanes], pot_in.at[pl.ds(8 * h, 8), :], load_sem.at[2 + h]))
    for c in loads:
        c.start()

    barrier = pltpu.get_barrier_semaphore()

    def greet(i, _):
        pl.semaphore_signal(barrier, inc=1, device_id=device(lax.rem(me + i, devices)), device_id_type=MESH)
        return 0

    lax.fori_loop(1, devices, greet, 0)

    for c in loads[2:]:
        c.wait()
    pots[my_place, my_plane] = pot_in[...] * (1.0 / HALF_WIDTH)
    pl.semaphore_wait(barrier, devices - 1)

    def copy_out(src, dst, sems, target):
        return pltpu.make_async_remote_copy(
            src_ref=src, dst_ref=dst, send_sem=sems[0], recv_sem=sems[1],
            device_id=device(target), device_id_type=MESH,
        )

    def drain(ref, sem):
        pltpu.make_async_copy(ref, ref, sem).wait()

    for step in range(1, planes):
        here = pots.at[my_place, my_plane]
        copy_out(here, here, (pot_send.at[0], pot_recv.at[0]), plane_peer(step)).start()

    stride = next(n for n in (13, 11, 7, 5, 3, 1) if math.gcd(n, devices) == 1)

    def send_psi(o):
        def body(i, _):
            target = lax.rem(me + i * stride, devices)
            copy_out(
                send.at[target * own + o], field.at[o, me],
                (psi_send.at[o], psi_recv.at[o]), target,
            ).start()
            return 0

        lax.fori_loop(1, devices, body, 0)
        field[o, me] = send[me * own + o]

    for c in loads[:2]:
        c.wait()
    send_psi(0)
    drain(pots.at[0, pl.ds(0, planes - 1)], pot_recv.at[0])
    drain(pots.at[0, pl.ds(0, planes - 1)], pot_send.at[0])
    for step in range(1, 8):
        here = pots.at[my_place]
        copy_out(here, here, (pot_send.at[1], pot_recv.at[1]), place_peer(step)).start()
    for o in range(1, own):
        send_psi(o)

    zmat = z_matrix()
    tiles = 2 * ny
    rows = 8 * nx
    low = lax.broadcasted_iota(jnp.int32, (rows, LANES), 1) < NZ
    weights = [-0.5 * c / HALF_WIDTH for c in COEFS]

    def tile_of(ref, o, t):
        return jnp.concatenate(
            [ref[o, b * ny + t // 2, 8 * (t % 2) : 8 * (t % 2) + 8, :] for b in range(nx)], axis=0
        )

    def pot_tile(t):
        parts = []
        for b in range(nx):
            d = b * ny + t // 2
            parts.append(pots[d % 8, d // 8, 8 * (t % 2) : 8 * (t % 2) + 8, :])
        return jnp.concatenate(parts, axis=0)

    def apply(src, emit):
        zpart[...] = dot_nn(work[src].reshape(tiles * rows, LANES), zmat).reshape(tiles, rows, LANES)
        for t in range(tiles):
            half[t] = pltpu.roll(work[src, t], NZ, 1)
        for t in range(tiles):
            v = work[src, t]
            total = zpart[t] + pot_tile(t) * v
            for d in range(1, 5):
                total = total + weights[d] * (pltpu.roll(v, d, 0) + pltpu.roll(v, rows - d, 0))
            total = total + weights[2] * (work[src, (t + 1) % tiles] + work[src, (t - 1) % tiles])
            total = total + weights[4] * (work[src, (t + 2) % tiles] + work[src, (t - 2) % tiles])
            s = [half[(t + k) % tiles] for k in range(-2, 3)]
            total = total + weights[1] * (s[2] + jnp.where(low, s[1], s[3]))
            total = total + weights[3] * jnp.where(low, s[3] + s[0], s[4] + s[1])
            emit(t, total)

    def send_back(o):
        def body(i, _):
            target = lax.rem(me + i * stride, devices)
            copy_out(
                back.at[o, target], block.at[pl.ds((me * own + o) * 16, 16)],
                (ret_send.at[o], ret_recv), target,
            ).start()
            return 0

        lax.fori_loop(1, devices, body, 0)
        block[pl.ds((me * own + o) * 16, 16), :] = back[o, me]

    for o in range(own):
        drain(field.at[o, pl.ds(0, devices - 1)], psi_recv.at[o])
        if o == 0:
            drain(pots.at[pl.ds(0, 7)], pot_recv.at[1])
        for t in range(tiles):
            work[0, t] = tile_of(field, o, t)

        def emit_one(t, value):
            work[1, t] = value

        def emit_two(t, value):
            work[2, t] = 2.0 * value - work[0, t]

        def emit_three(t, value):
            value = 2.0 * value - work[1, t]
            for b in range(nx):
                back[o, b * ny + t // 2, 8 * (t % 2) : 8 * (t % 2) + 8, :] = value[8 * b : 8 * b + 8]

        apply(0, emit_one)
        apply(1, emit_two)
        apply(2, emit_three)
        send_back(o)

    drain(pots.at[pl.ds(0, 7)], pot_send.at[1])
    for o in range(own):
        drain(field.at[o, pl.ds(0, devices - 1)], psi_send.at[o])
        drain(back.at[o, pl.ds(0, devices - 1)], ret_send.at[o])
    drain(block.at[pl.ds(0, (devices - 1) * own * 16)], ret_recv)

    for j in range(16):
        matrix[:, j * LANES : (j + 1) * LANES] = block[pl.ds(j, orbits, stride=16), :]

    ncount = float(rows * tiles * LANES)
    halfrows = orbits // 2

    def total_gram(turn, local):
        local = jnp.concatenate([local[:halfrows], local[halfrows:]], axis=1)
        sum_a[turn, my_plane] = local
        for step in range(1, planes):
            here = sum_a.at[turn, my_plane]
            copy_out(here, here, (sum_send.at[turn, 0], sum_recv.at[turn, 0]), plane_peer(step)).start()
        drain(sum_a.at[turn, pl.ds(0, planes - 1)], sum_recv.at[turn, 0])
        drain(sum_a.at[turn, pl.ds(0, planes - 1)], sum_send.at[turn, 0])
        total = sum_a[turn, 0]
        for i in range(1, planes):
            total = total + sum_a[turn, i]
        sum_b[turn, my_place] = total
        for step in range(1, 8):
            here = sum_b.at[turn, my_place]
            copy_out(here, here, (sum_send.at[turn, 1], sum_recv.at[turn, 1]), place_peer(step)).start()
        drain(sum_b.at[turn, pl.ds(0, 7)], sum_recv.at[turn, 1])
        drain(sum_b.at[turn, pl.ds(0, 7)], sum_send.at[turn, 1])
        total = sum_b[turn, 0]
        for i in range(1, 8):
            total = total + sum_b[turn, i]
        total = total * (1.0 / ncount)
        return jnp.concatenate([total[:, :orbits], total[:, orbits:]], axis=0)

    for turn in range(2):
        x = matrix[...]
        gram = total_gram(turn, dot_nt(x, x))
        matrix[...] = dot_nn(inverse_factor(gram), matrix[...])
    for j in range(16):
        block[pl.ds(j, orbits, stride=16), :] = matrix[:, j * LANES : (j + 1) * LANES]
    for m in range(orbits):
        for h in range(2):
            out_ref[m, :, h * LANES : (h + 1) * LANES] = block[16 * m + 8 * h : 16 * m + 8 * h + 8, :]


def transposed(nx, ny, psi, potential):
    orbits = psi.shape[0]
    devices = nx * ny
    own = orbits // devices
    f32 = jnp.float32
    tiles, rows = 2 * ny, 8 * nx
    dma = pltpu.SemaphoreType.DMA
    return pl.pallas_call(
        functools.partial(kernel, nx, ny),
        out_shape=jax.ShapeDtypeStruct(psi.shape, f32),
        in_specs=[pl.BlockSpec(memory_space=pl.ANY)] * 2,
        out_specs=pl.BlockSpec(memory_space=pltpu.VMEM),
        scratch_shapes=[
            pltpu.VMEM((orbits, 16, LANES), f32),
            pltpu.VMEM((own, devices, 16, LANES), f32),
            pltpu.VMEM((8, devices // 8, 16, LANES), f32),
            pltpu.VMEM((3, tiles, rows, LANES), f32),
            pltpu.VMEM((tiles, rows, LANES), f32),
            pltpu.VMEM((tiles, rows, LANES), f32),
            pltpu.VMEM((own, devices, 16, LANES), f32),
            pltpu.VMEM((orbits * 16, LANES), f32),
            pltpu.VMEM((orbits, 16 * LANES), f32),
            pltpu.VMEM((16, LANES), f32),
            pltpu.VMEM((2, devices // 8, orbits // 2, 2 * orbits), f32),
            pltpu.VMEM((2, 8, orbits // 2, 2 * orbits), f32),
            dma((4,)), dma((own,)), dma((own,)), dma((own,)), dma,
            dma((2,)), dma((2,)), dma((2, 2)), dma((2, 2)),
        ],
        compiler_params=pltpu.CompilerParams(
            collective_id=0, has_side_effects=True
        ),
    )(psi, potential)


def solution(mesh):
    in_specs = (P(None, "gx", "gy"), P("gx", "gy"))
    out_specs = P(None, "gx", "gy")
    nx, ny = mesh.shape["gx"], mesh.shape["gy"]

    def step(psi, potential):
        orbits, rows, lanes = psi.shape
        whole_orbits = orbits % (nx * ny) == 0 and (nx * ny) % 16 == 0
        if whole_orbits and rows == 8 and lanes == 2 * LANES and orbits == 64 and ny >= 4:
            return transposed(nx, ny, psi, potential)
        return on_device(psi, potential)

    return jax.shard_map(step, mesh=mesh, in_specs=in_specs, out_specs=out_specs, check_vma=False)
```

```python
import functools
import math

import jax
import jax.numpy as jnp
from jax import lax
from jax.experimental import pallas as pl
from jax.experimental.pallas import tpu as pltpu
from jax.sharding import PartitionSpec as P

NZ = 64


COEFS = (-205.0 / 72.0, 8.0 / 5.0, -1.0 / 5.0, 8.0 / 315.0, -1.0 / 560.0)
CENTER = 6.5
HALF_WIDTH = 5.5


def padded(array, sides, width):
    for axis, dim in sides:
        size, length = (lax.axis_size(axis), array.shape[dim])
        up = [(i, (i + 1) % size) for i in range(size)]
        down = [(j, i) for i, j in up]
        last = lax.slice_in_dim(array, length - width, length, axis=dim)
        first = lax.slice_in_dim(array, 0, width, axis=dim)
        before = lax.ppermute(last, axis, up)
        after = lax.ppermute(first, axis, down)
        array = jnp.concatenate([before, array, after], axis=dim)
    return array


def along_third(field, depth_index):
    laplace = 3.0 * COEFS[0] * field
    for distance in range(1, 5):
        forward = jnp.where(
            depth_index < NZ - distance,
            jnp.roll(field, -distance, 2),
            jnp.roll(field, NZ - distance, 2),
        )
        behind = jnp.where(
            depth_index >= distance, jnp.roll(field, distance, 2), jnp.roll(field, distance - NZ, 2)
        )
        laplace = laplace + COEFS[distance] * (forward + behind)
    return laplace


def hamiltonian(field, field_pot, depth_index):
    row_count = field.shape[1]
    lane_count = field.shape[2]
    padded_x = padded(field, (("gx", 1),), 4)
    laplace = along_third(field, depth_index)
    padded_y = padded(field, (("gy", 2),), 4 * NZ)
    for distance in range(1, 5):
        laplace = laplace + COEFS[distance] * (
            padded_x[:, 4 + distance : 4 + distance + row_count]
            + padded_x[:, 4 - distance : 4 - distance + row_count]
        )
        ahead_start = (4 + distance) * NZ
        back_start = (4 - distance) * NZ
        laplace = laplace + COEFS[distance] * (
            padded_y[:, :, ahead_start : ahead_start + lane_count]
            + padded_y[:, :, back_start : back_start + lane_count]
        )
    return -0.5 * laplace + field_pot * field


def orthonormal(matrix, ncount):
    local_gram = jnp.dot(matrix, matrix.T, precision=lax.Precision.HIGHEST) / ncount
    total_gram = lax.psum(local_gram, ("gx", "gy"))
    lower_factor = jnp.linalg.cholesky(total_gram)
    return lax.linalg.triangular_solve(lower_factor, matrix, left_side=True, lower=True)


def on_device(psi, potential):
    orbit_count = psi.shape[0]
    row_count = psi.shape[1]
    lane_count = psi.shape[2]
    field_pot = potential.reshape(1, row_count, lane_count)
    depth_index = lax.broadcasted_iota(jnp.int32, (1, 1, lane_count), 2) % NZ
    level_one = (hamiltonian(psi, field_pot, depth_index) - CENTER * psi) / HALF_WIDTH
    second = (
        2.0 * (hamiltonian(level_one, field_pot, depth_index) - CENTER * level_one) / HALF_WIDTH
        - psi
    )
    filtered = (
        2.0 * (hamiltonian(second, field_pot, depth_index) - CENTER * second) / HALF_WIDTH
        - level_one
    )
    matrix = filtered.reshape(orbit_count, row_count * lane_count)
    ncount = float(row_count * lane_count * lax.axis_size("gx") * lax.axis_size("gy"))
    first_pass = orthonormal(matrix, ncount)
    final_pass = orthonormal(first_pass, ncount)
    return final_pass.reshape(orbit_count, row_count, lane_count)


MESH = pl.DeviceIdType.MESH
EXACT = lax.Precision.HIGHEST
LANES = 128


def z_matrix():
    row = lax.broadcasted_iota(jnp.int32, (LANES, LANES), 0)
    col = lax.broadcasted_iota(jnp.int32, (LANES, LANES), 1)
    same = (row // NZ) == (col // NZ)
    gap = (row - col + 2 * NZ) % NZ
    gap = jnp.minimum(gap, NZ - gap)
    matrix = jnp.zeros((LANES, LANES), jnp.float32)
    for distance in range(5):
        if distance == 0:
            value = (-1.5 * COEFS[0] - CENTER) / HALF_WIDTH
        else:
            value = -0.5 * COEFS[distance] / HALF_WIDTH
        matrix = jnp.where(same & (gap == distance), value, matrix)
    return matrix


def dot_nn(a, b):
    return lax.dot_general(a, b, (((1,), (0,)), ((), ())), precision=EXACT, preferred_element_type=jnp.float32)


def dot_nt(a, b):
    return lax.dot_general(a, b, (((1,), (1,)), ((), ())), precision=EXACT, preferred_element_type=jnp.float32)


def inverse_factor(gram):
    tiles = len(gram)
    count = 8 * tiles
    shape = (8, 2 * count)
    row_in = lax.broadcasted_iota(jnp.int32, shape, 0)
    lane = lax.broadcasted_iota(jnp.int32, shape, 1)
    blocks = []
    for i in range(tiles):
        eye = jnp.where(lane == row_in + 8 * i + count, 1.0, 0.0)
        blocks.append(jnp.where(lane < count, gram[i], eye))

    def row_of(array, j):
        return jnp.broadcast_to(array[j : j + 1, :], shape)

    out = []
    for t in range(tiles):
        cols = [[jnp.broadcast_to(blocks[i][:, 8 * t + j : 8 * t + j + 1], shape) for j in range(8)] for i in range(t, tiles)]
        diag = [[row_of(cols[0][j], a) if a >= j else None for j in range(8)] for a in range(8)]
        inverse, pivots = [], []
        factor = [[None] * 8 for _ in range(8)]
        for j in range(8):
            pivots.append(diag[j][j])
            guess = pl.reciprocal(diag[j][j], approx=True)
            guess = guess * (2.0 - diag[j][j] * guess)
            inverse.append(guess * (2.0 - diag[j][j] * guess))
            for a in range(j + 1, 8):
                factor[a][j] = diag[a][j] * inverse[j]
            for a in range(j + 1, 8):
                for b in range(j + 1, a + 1):
                    diag[a][b] = diag[a][b] - factor[a][j] * diag[b][j]
        current = blocks[t]
        finished = []
        for j in range(8):
            finished.append(row_of(current, j))
            if j < 7:
                below = jnp.zeros(shape, jnp.float32)
                for a in range(j + 1, 8):
                    below = jnp.where(row_in == a, factor[a][j], below)
                current = current - below * finished[j]
        blocks[t] = current
        for i in range(t + 1, tiles):
            col = cols[i - t]
            total = blocks[i]
            for j in range(8):
                scaled = col[j] * inverse[j]
                total = total - scaled * finished[j]
                for b in range(j + 1, 8):
                    col[b] = col[b] - scaled * diag[b][j]
            blocks[i] = total
        pivot = pivots[0]
        for j in range(1, 8):
            pivot = jnp.where(row_in == j, pivots[j], pivot)
        out.append((current / jnp.sqrt(pivot))[:, count:])
    return jnp.concatenate(out, axis=0)


def kernel(
    nx, ny, psi_ref, pot_ref, first_ref, factor_ref,
    send, field, pots, work, half, zpart, back, block, matrix, pot_in, sum_out, sum_a, sum_b, sum_c, load_sem,
    psi_send, psi_recv, ret_send, ret_recv, pot_send, pot_recv, sum_send, sum_recv,
):
    devices = nx * ny
    orbits = psi_ref.shape[0]
    own = orbits // devices
    planes = devices // 8
    me = lax.axis_index("gx") * ny + lax.axis_index("gy")
    my_plane, my_place = me // 8, me % 8

    def device(target):
        return (target // ny, target % ny)

    def place_peer(step):
        return my_plane * 8 + lax.rem(my_place + step, 8)

    def plane_peer(step):
        return lax.rem(my_plane + step, planes) * 8 + my_place

    loads = []
    for h in range(2):
        half_lanes = pl.ds(h * LANES, LANES)
        loads.append(pltpu.make_async_copy(
            psi_ref.at[:, :, half_lanes], send.at[:, pl.ds(8 * h, 8), :], load_sem.at[h]))
    for h in range(2):
        half_lanes = pl.ds(h * LANES, LANES)
        loads.append(pltpu.make_async_copy(
            pot_ref.at[:, half_lanes], pot_in.at[pl.ds(8 * h, 8), :], load_sem.at[2 + h]))
    for c in loads:
        c.start()

    barrier = pltpu.get_barrier_semaphore()

    def greet(i, _):
        pl.semaphore_signal(barrier, inc=1, device_id=device(lax.rem(me + i, devices)), device_id_type=MESH)
        return 0

    lax.fori_loop(1, devices, greet, 0)

    for c in loads[2:]:
        c.wait()
    pots[my_place, my_plane] = pot_in[...] * (1.0 / HALF_WIDTH)
    pl.semaphore_wait(barrier, devices - 1)

    def copy_out(src, dst, sems, target):
        return pltpu.make_async_remote_copy(
            src_ref=src, dst_ref=dst, send_sem=sems[0], recv_sem=sems[1],
            device_id=device(target), device_id_type=MESH,
        )

    def drain(ref, sem):
        pltpu.make_async_copy(ref, ref, sem).wait()

    for step in range(1, planes):
        here = pots.at[my_place, my_plane]
        copy_out(here, here, (pot_send.at[0], pot_recv.at[0]), plane_peer(step)).start()

    stride = next(n for n in (13, 11, 7, 5, 3, 1) if math.gcd(n, devices) == 1)

    def send_psi(o):
        def body(i, _):
            target = lax.rem(me + i * stride, devices)
            copy_out(
                send.at[target * own + o], field.at[o, me],
                (psi_send.at[o], psi_recv.at[o]), target,
            ).start()
            return 0

        lax.fori_loop(1, devices, body, 0)
        field[o, me] = send[me * own + o]

    for c in loads[:2]:
        c.wait()
    send_psi(0)
    drain(pots.at[0, pl.ds(0, planes - 1)], pot_recv.at[0])
    drain(pots.at[0, pl.ds(0, planes - 1)], pot_send.at[0])
    for step in range(1, 8):
        here = pots.at[my_place]
        copy_out(here, here, (pot_send.at[1], pot_recv.at[1]), place_peer(step)).start()
    for o in range(1, own):
        send_psi(o)

    zmat = z_matrix()
    tiles = 2 * ny
    rows = 8 * nx
    low = lax.broadcasted_iota(jnp.int32, (rows, LANES), 1) < NZ
    weights = [-0.5 * c / HALF_WIDTH for c in COEFS]

    def tile_of(ref, o, t):
        return jnp.concatenate(
            [ref[o, b * ny + t // 2, 8 * (t % 2) : 8 * (t % 2) + 8, :] for b in range(nx)], axis=0
        )

    def pot_tile(t):
        parts = []
        for b in range(nx):
            d = b * ny + t // 2
            parts.append(pots[d % 8, d // 8, 8 * (t % 2) : 8 * (t % 2) + 8, :])
        return jnp.concatenate(parts, axis=0)

    def apply(src, emit):
        zpart[...] = dot_nn(work[src].reshape(tiles * rows, LANES), zmat).reshape(tiles, rows, LANES)
        for t in range(tiles):
            half[t] = pltpu.roll(work[src, t], NZ, 1)
        for t in range(tiles):
            v = work[src, t]
            total = zpart[t] + pot_tile(t) * v
            for d in range(1, 5):
                total = total + weights[d] * (pltpu.roll(v, d, 0) + pltpu.roll(v, rows - d, 0))
            total = total + weights[2] * (work[src, (t + 1) % tiles] + work[src, (t - 1) % tiles])
            total = total + weights[4] * (work[src, (t + 2) % tiles] + work[src, (t - 2) % tiles])
            s = [half[(t + k) % tiles] for k in range(-2, 3)]
            total = total + weights[1] * (s[2] + jnp.where(low, s[1], s[3]))
            total = total + weights[3] * jnp.where(low, s[3] + s[0], s[4] + s[1])
            emit(t, total)

    def send_back(o):
        def body(i, _):
            target = lax.rem(me + i * stride, devices)
            copy_out(
                back.at[o, target], block.at[pl.ds((me * own + o) * 16, 16)],
                (ret_send.at[o], ret_recv), target,
            ).start()
            return 0

        lax.fori_loop(1, devices, body, 0)
        block[pl.ds((me * own + o) * 16, 16), :] = back[o, me]

    for o in range(own):
        drain(field.at[o, pl.ds(0, devices - 1)], psi_recv.at[o])
        if o == 0:
            drain(pots.at[pl.ds(0, 7)], pot_recv.at[1])
        for t in range(tiles):
            work[0, t] = tile_of(field, o, t)

        def emit_one(t, value):
            work[1, t] = value

        def emit_two(t, value):
            work[2, t] = 2.0 * value - work[0, t]

        def emit_three(t, value):
            value = 2.0 * value - work[1, t]
            for b in range(nx):
                back[o, b * ny + t // 2, 8 * (t % 2) : 8 * (t % 2) + 8, :] = value[8 * b : 8 * b + 8]

        apply(0, emit_one)
        apply(1, emit_two)
        apply(2, emit_three)
        send_back(o)

    drain(block.at[pl.ds(0, (devices - 1) * own * 16)], ret_recv)

    for j in range(16):
        matrix[:, j * LANES : (j + 1) * LANES] = block[pl.ds(j, orbits, stride=16), :]

    ncount = float(rows * tiles * LANES)
    pieces = orbits // 8

    def total_gram(turn, local):
        local = jnp.concatenate([local, jnp.zeros_like(local)], axis=1)
        for p in range(pieces):
            sum_out[turn, p] = local[8 * p : 8 * p + 8]
        for step in range(1, 8):
            peer = lax.rem(my_place + step, 8)
            copy_out(
                sum_out.at[turn, peer], sum_a.at[turn, my_place],
                (sum_send.at[turn, 0], sum_recv.at[turn, 0]), my_plane * 8 + peer,
            ).start()
        sum_a[turn, my_place] = sum_out[turn, my_place]
        drain(sum_a.at[turn, pl.ds(0, 7)], sum_recv.at[turn, 0])
        total = sum_a[turn, 0]
        for i in range(1, 8):
            total = total + sum_a[turn, i]
        sum_b[turn, my_plane] = total
        for step in range(1, planes):
            here = sum_b.at[turn, my_plane]
            copy_out(here, here, (sum_send.at[turn, 1], sum_recv.at[turn, 1]), plane_peer(step)).start()
        drain(sum_b.at[turn, pl.ds(0, planes - 1)], sum_recv.at[turn, 1])
        total = sum_b[turn, 0]
        for i in range(1, planes):
            total = total + sum_b[turn, i]
        sum_c[turn, my_place] = total * (1.0 / ncount)
        for step in range(1, 8):
            here = sum_c.at[turn, my_place]
            copy_out(here, here, (sum_send.at[turn, 2], sum_recv.at[turn, 2]), place_peer(step)).start()
        drain(sum_c.at[turn, pl.ds(0, 7)], sum_recv.at[turn, 2])
        return [sum_c[turn, p] for p in range(pieces)]

    x = matrix[...]
    gram = total_gram(0, dot_nt(x, x))
    matrix[...] = dot_nn(inverse_factor(gram), matrix[...])
    store = pltpu.make_async_copy(matrix, first_ref, load_sem.at[0])
    store.start()
    x = matrix[...]
    gram = total_gram(1, dot_nt(x, x))
    factor_ref[...] = inverse_factor(gram)

    store.wait()
    drain(pots.at[pl.ds(0, 7)], pot_send.at[1])
    for o in range(own):
        drain(field.at[o, pl.ds(0, devices - 1)], psi_send.at[o])
        drain(back.at[o, pl.ds(0, devices - 1)], ret_send.at[o])
    for turn in range(2):
        drain(sum_a.at[turn, pl.ds(0, 7)], sum_send.at[turn, 0])
        drain(sum_b.at[turn, pl.ds(0, planes - 1)], sum_send.at[turn, 1])
        drain(sum_c.at[turn, pl.ds(0, 7)], sum_send.at[turn, 2])


def finish(factor_ref, first_ref, out_ref):
    orbits = factor_ref.shape[0]
    value = dot_nn(factor_ref[...], first_ref[...])
    flat = out_ref.reshape(orbits * 8, LANES)
    for r in range(8):
        flat[pl.ds(r, orbits, stride=8), :] = value[:, r * LANES : (r + 1) * LANES]


def transposed(nx, ny, psi, potential):
    orbits = psi.shape[0]
    devices = nx * ny
    own = orbits // devices
    f32 = jnp.float32
    tiles, rows = 2 * ny, 8 * nx
    dma = pltpu.SemaphoreType.DMA
    first, factor = pl.pallas_call(
        functools.partial(kernel, nx, ny),
        out_shape=(
            jax.ShapeDtypeStruct((orbits, 16 * LANES), f32),
            jax.ShapeDtypeStruct((orbits, orbits), f32),
        ),
        in_specs=[pl.BlockSpec(memory_space=pl.ANY)] * 2,
        out_specs=(pl.BlockSpec(memory_space=pl.ANY), pl.BlockSpec(memory_space=pltpu.VMEM)),
        scratch_shapes=[
            pltpu.VMEM((orbits, 16, LANES), f32),
            pltpu.VMEM((own, devices, 16, LANES), f32),
            pltpu.VMEM((8, devices // 8, 16, LANES), f32),
            pltpu.VMEM((3, tiles, rows, LANES), f32),
            pltpu.VMEM((tiles, rows, LANES), f32),
            pltpu.VMEM((tiles, rows, LANES), f32),
            pltpu.VMEM((own, devices, 16, LANES), f32),
            pltpu.VMEM((orbits * 16, LANES), f32),
            pltpu.VMEM((orbits, 16 * LANES), f32),
            pltpu.VMEM((16, LANES), f32),
            pltpu.VMEM((2, 8, 8, LANES), f32),
            pltpu.VMEM((2, 8, 8, LANES), f32),
            pltpu.VMEM((2, devices // 8, 8, LANES), f32),
            pltpu.VMEM((2, 8, 8, LANES), f32),
            dma((4,)), dma((own,)), dma((own,)), dma((own,)), dma,
            dma((2,)), dma((2,)), dma((2, 3)), dma((2, 3)),
        ],
        compiler_params=pltpu.CompilerParams(
            collective_id=0, has_side_effects=True
        ),
    )(psi, potential)
    return pl.pallas_call(
        finish,
        grid=(2,),
        out_shape=jax.ShapeDtypeStruct(psi.shape, f32),
        in_specs=[
            pl.BlockSpec((orbits, orbits), lambda h: (0, 0)),
            pl.BlockSpec((orbits, 8 * LANES), lambda h: (0, h)),
        ],
        out_specs=pl.BlockSpec((orbits, 8, LANES), lambda h: (0, 0, h)),
    )(factor, first)


def solution(mesh):
    in_specs = (P(None, "gx", "gy"), P("gx", "gy"))
    out_specs = P(None, "gx", "gy")
    nx, ny = mesh.shape["gx"], mesh.shape["gy"]

    def step(psi, potential):
        orbits, rows, lanes = psi.shape
        whole_orbits = orbits % (nx * ny) == 0 and (nx * ny) % 16 == 0
        if whole_orbits and rows == 8 and lanes == 2 * LANES and orbits == 64 and ny >= 4:
            return transposed(nx, ny, psi, potential)
        return on_device(psi, potential)

    return jax.shard_map(step, mesh=mesh, in_specs=in_specs, out_specs=out_specs, check_vma=False)
```

```python
import functools
import math

import jax
import jax.numpy as jnp
from jax import lax
from jax.experimental import pallas as pl
from jax.experimental.pallas import tpu as pltpu
from jax.sharding import PartitionSpec as P

NZ = 64


COEFS = (-205.0 / 72.0, 8.0 / 5.0, -1.0 / 5.0, 8.0 / 315.0, -1.0 / 560.0)
CENTER = 6.5
HALF_WIDTH = 5.5


def padded(array, sides, width):
    for axis, dim in sides:
        size, length = (lax.axis_size(axis), array.shape[dim])
        up = [(i, (i + 1) % size) for i in range(size)]
        down = [(j, i) for i, j in up]
        last = lax.slice_in_dim(array, length - width, length, axis=dim)
        first = lax.slice_in_dim(array, 0, width, axis=dim)
        before = lax.ppermute(last, axis, up)
        after = lax.ppermute(first, axis, down)
        array = jnp.concatenate([before, array, after], axis=dim)
    return array


def along_third(field, depth_index):
    laplace = 3.0 * COEFS[0] * field
    for distance in range(1, 5):
        forward = jnp.where(
            depth_index < NZ - distance,
            jnp.roll(field, -distance, 2),
            jnp.roll(field, NZ - distance, 2),
        )
        behind = jnp.where(
            depth_index >= distance, jnp.roll(field, distance, 2), jnp.roll(field, distance - NZ, 2)
        )
        laplace = laplace + COEFS[distance] * (forward + behind)
    return laplace


def hamiltonian(field, field_pot, depth_index):
    row_count = field.shape[1]
    lane_count = field.shape[2]
    padded_x = padded(field, (("gx", 1),), 4)
    laplace = along_third(field, depth_index)
    padded_y = padded(field, (("gy", 2),), 4 * NZ)
    for distance in range(1, 5):
        laplace = laplace + COEFS[distance] * (
            padded_x[:, 4 + distance : 4 + distance + row_count]
            + padded_x[:, 4 - distance : 4 - distance + row_count]
        )
        ahead_start = (4 + distance) * NZ
        back_start = (4 - distance) * NZ
        laplace = laplace + COEFS[distance] * (
            padded_y[:, :, ahead_start : ahead_start + lane_count]
            + padded_y[:, :, back_start : back_start + lane_count]
        )
    return -0.5 * laplace + field_pot * field


def orthonormal(matrix, ncount):
    local_gram = jnp.dot(matrix, matrix.T, precision=lax.Precision.HIGHEST) / ncount
    total_gram = lax.psum(local_gram, ("gx", "gy"))
    lower_factor = jnp.linalg.cholesky(total_gram)
    return lax.linalg.triangular_solve(lower_factor, matrix, left_side=True, lower=True)


def on_device(psi, potential):
    orbit_count = psi.shape[0]
    row_count = psi.shape[1]
    lane_count = psi.shape[2]
    field_pot = potential.reshape(1, row_count, lane_count)
    depth_index = lax.broadcasted_iota(jnp.int32, (1, 1, lane_count), 2) % NZ
    level_one = (hamiltonian(psi, field_pot, depth_index) - CENTER * psi) / HALF_WIDTH
    second = (
        2.0 * (hamiltonian(level_one, field_pot, depth_index) - CENTER * level_one) / HALF_WIDTH
        - psi
    )
    filtered = (
        2.0 * (hamiltonian(second, field_pot, depth_index) - CENTER * second) / HALF_WIDTH
        - level_one
    )
    matrix = filtered.reshape(orbit_count, row_count * lane_count)
    ncount = float(row_count * lane_count * lax.axis_size("gx") * lax.axis_size("gy"))
    first_pass = orthonormal(matrix, ncount)
    final_pass = orthonormal(first_pass, ncount)
    return final_pass.reshape(orbit_count, row_count, lane_count)


MESH = pl.DeviceIdType.MESH
EXACT = lax.Precision.HIGHEST
LANES = 128


def z_matrix():
    row = lax.broadcasted_iota(jnp.int32, (LANES, LANES), 0)
    col = lax.broadcasted_iota(jnp.int32, (LANES, LANES), 1)
    same = (row // NZ) == (col // NZ)
    gap = (row - col + 2 * NZ) % NZ
    gap = jnp.minimum(gap, NZ - gap)
    matrix = jnp.zeros((LANES, LANES), jnp.float32)
    for distance in range(5):
        if distance == 0:
            value = (-1.5 * COEFS[0] - CENTER) / HALF_WIDTH
        else:
            value = -0.5 * COEFS[distance] / HALF_WIDTH
        matrix = jnp.where(same & (gap == distance), value, matrix)
    return matrix


def dot_nn(a, b):
    return lax.dot_general(a, b, (((1,), (0,)), ((), ())), precision=EXACT, preferred_element_type=jnp.float32)


def dot_nt(a, b):
    return lax.dot_general(a, b, (((1,), (1,)), ((), ())), precision=EXACT, preferred_element_type=jnp.float32)


def inverse_factor(gram):
    tiles = len(gram)
    count = 8 * tiles
    shape = (8, 2 * count)
    row_in = lax.broadcasted_iota(jnp.int32, shape, 0)
    lane = lax.broadcasted_iota(jnp.int32, shape, 1)
    blocks = []
    for i in range(tiles):
        eye = jnp.where(lane == row_in + 8 * i + count, 1.0, 0.0)
        blocks.append(jnp.where(lane < count, gram[i], eye))

    def row_of(array, j):
        return jnp.broadcast_to(array[j : j + 1, :], shape)

    out = []
    for t in range(tiles):
        cols = [[jnp.broadcast_to(blocks[i][:, 8 * t + j : 8 * t + j + 1], shape) for j in range(8)] for i in range(t, tiles)]
        diag = [[row_of(cols[0][j], a) if a >= j else None for j in range(8)] for a in range(8)]
        inverse, pivots = [], []
        factor = [[None] * 8 for _ in range(8)]
        for j in range(8):
            pivots.append(diag[j][j])
            guess = pl.reciprocal(diag[j][j], approx=True)
            guess = guess * (2.0 - diag[j][j] * guess)
            inverse.append(guess * (2.0 - diag[j][j] * guess))
            for a in range(j + 1, 8):
                factor[a][j] = diag[a][j] * inverse[j]
            for a in range(j + 1, 8):
                for b in range(j + 1, a + 1):
                    diag[a][b] = diag[a][b] - factor[a][j] * diag[b][j]
        current = blocks[t]
        finished = []
        for j in range(8):
            finished.append(row_of(current, j))
            if j < 7:
                below = jnp.zeros(shape, jnp.float32)
                for a in range(j + 1, 8):
                    below = jnp.where(row_in == a, factor[a][j], below)
                current = current - below * finished[j]
        blocks[t] = current
        for i in range(t + 1, tiles):
            col = cols[i - t]
            total = blocks[i]
            for j in range(8):
                scaled = col[j] * inverse[j]
                total = total - scaled * finished[j]
                for b in range(j + 1, 8):
                    col[b] = col[b] - scaled * diag[b][j]
            blocks[i] = total
        pivot = pivots[0]
        for j in range(1, 8):
            pivot = jnp.where(row_in == j, pivots[j], pivot)
        out.append((current / jnp.sqrt(pivot))[:, count:])
    return jnp.concatenate(out, axis=0)


def two_sum(a, b):
    total = a + b
    part = total - a
    return total, (a - (total - part)) + (b - part)


def pair_add(first, second):
    total, rest = two_sum(first[0], second[0])
    return total, rest + (first[1] + second[1])


def settle(pair):
    total = pair[0] + pair[1]
    return total, pair[1] - (total - pair[0])


def slices(pair, count):
    value, rest = pair
    size = jnp.max(jnp.abs(value), axis=1, keepdims=True) * 2.0**17
    out = []
    for p in range(count):
        if p == 3 and rest is not None:
            value = value + rest
        unit = size * 2.0 ** (-7 * p)
        term = (value + unit) - unit
        out.append(term.astype(jnp.bfloat16))
        value = value - term
    return out


def exact_products(left, right, depth):
    rows, total = left[0].shape
    stacked = jnp.concatenate(left, axis=0)
    pair = None
    for start in range(0, total, depth):
        orders = {}
        for q in range(0, len(right), 2):
            other = jnp.concatenate(right[q : q + 2], axis=0)
            product = lax.dot_general(
                stacked[:, start : start + depth], other[:, start : start + depth],
                (((1,), (1,)), ((), ())), preferred_element_type=jnp.float32,
            )
            for p in range(len(left)):
                block = product[rows * p : rows * p + rows]
                orders[p + q] = orders[p + q] + block if p + q in orders else block
        for order in sorted(orders):
            if pair is None:
                pair = orders[order], jnp.zeros_like(orders[order])
            else:
                value, rest = two_sum(pair[0], orders[order])
                pair = value, pair[1] + rest
    turned = pltpu.roll(pair[0], rows, 1), pltpu.roll(pair[1], rows, 1)
    return settle(pair_add(pair, turned))


def kernel(
    nx, ny, psi_ref, pot_ref, first_ref, factor_ref,
    send, field, pots, work, half, zpart, back, block, matrix, pot_in, sum_a, sum_b, load_sem,
    psi_send, psi_recv, ret_send, ret_recv, pot_send, pot_recv, sum_send, sum_recv,
):
    devices = nx * ny
    orbits = psi_ref.shape[0]
    own = orbits // devices
    planes = devices // 8
    me = lax.axis_index("gx") * ny + lax.axis_index("gy")
    my_plane, my_place = me // 8, me % 8

    def device(target):
        return (target // ny, target % ny)

    def place_peer(step):
        return my_plane * 8 + lax.rem(my_place + step, 8)

    def plane_peer(step):
        return lax.rem(my_plane + step, planes) * 8 + my_place

    loads = []
    for h in range(2):
        half_lanes = pl.ds(h * LANES, LANES)
        loads.append(pltpu.make_async_copy(
            psi_ref.at[:, :, half_lanes], send.at[:, pl.ds(8 * h, 8), :], load_sem.at[h]))
    for h in range(2):
        half_lanes = pl.ds(h * LANES, LANES)
        loads.append(pltpu.make_async_copy(
            pot_ref.at[:, half_lanes], pot_in.at[pl.ds(8 * h, 8), :], load_sem.at[2 + h]))
    for c in loads:
        c.start()

    barrier = pltpu.get_barrier_semaphore()

    def greet(i, _):
        pl.semaphore_signal(barrier, inc=1, device_id=device(lax.rem(me + i, devices)), device_id_type=MESH)
        return 0

    lax.fori_loop(1, devices, greet, 0)

    for c in loads[2:]:
        c.wait()
    pots[my_place, my_plane] = pot_in[...] * (1.0 / HALF_WIDTH)
    pl.semaphore_wait(barrier, devices - 1)

    def copy_out(src, dst, sems, target):
        return pltpu.make_async_remote_copy(
            src_ref=src, dst_ref=dst, send_sem=sems[0], recv_sem=sems[1],
            device_id=device(target), device_id_type=MESH,
        )

    def drain(ref, sem):
        pltpu.make_async_copy(ref, ref, sem).wait()

    for step in range(1, planes):
        here = pots.at[my_place, my_plane]
        copy_out(here, here, (pot_send.at[0], pot_recv.at[0]), plane_peer(step)).start()

    stride = next(n for n in (13, 11, 7, 5, 3, 1) if math.gcd(n, devices) == 1)

    def send_psi(o):
        def body(i, _):
            target = lax.rem(me + i * stride, devices)
            copy_out(
                send.at[target * own + o], field.at[o, me],
                (psi_send.at[o], psi_recv.at[o]), target,
            ).start()
            return 0

        lax.fori_loop(1, devices, body, 0)
        field[o, me] = send[me * own + o]

    for c in loads[:2]:
        c.wait()
    send_psi(0)
    drain(pots.at[0, pl.ds(0, planes - 1)], pot_recv.at[0])
    drain(pots.at[0, pl.ds(0, planes - 1)], pot_send.at[0])
    for step in range(1, 8):
        here = pots.at[my_place]
        copy_out(here, here, (pot_send.at[1], pot_recv.at[1]), place_peer(step)).start()
    for o in range(1, own):
        send_psi(o)

    zmat = z_matrix()
    tiles = 2 * ny
    rows = 8 * nx
    low = lax.broadcasted_iota(jnp.int32, (rows, LANES), 1) < NZ
    weights = [-0.5 * c / HALF_WIDTH for c in COEFS]

    def tile_of(ref, o, t):
        return jnp.concatenate(
            [ref[o, b * ny + t // 2, 8 * (t % 2) : 8 * (t % 2) + 8, :] for b in range(nx)], axis=0
        )

    def pot_tile(t):
        parts = []
        for b in range(nx):
            d = b * ny + t // 2
            parts.append(pots[d % 8, d // 8, 8 * (t % 2) : 8 * (t % 2) + 8, :])
        return jnp.concatenate(parts, axis=0)

    def apply(src, emit):
        zpart[...] = dot_nn(work[src].reshape(tiles * rows, LANES), zmat).reshape(tiles, rows, LANES)
        for t in range(tiles):
            half[t] = pltpu.roll(work[src, t], NZ, 1)
        for t in range(tiles):
            v = work[src, t]
            total = zpart[t] + pot_tile(t) * v
            for d in range(1, 5):
                total = total + weights[d] * (pltpu.roll(v, d, 0) + pltpu.roll(v, rows - d, 0))
            total = total + weights[2] * (work[src, (t + 1) % tiles] + work[src, (t - 1) % tiles])
            total = total + weights[4] * (work[src, (t + 2) % tiles] + work[src, (t - 2) % tiles])
            s = [half[(t + k) % tiles] for k in range(-2, 3)]
            total = total + weights[1] * (s[2] + jnp.where(low, s[1], s[3]))
            total = total + weights[3] * jnp.where(low, s[3] + s[0], s[4] + s[1])
            emit(t, total)

    def send_back(o):
        def body(i, _):
            target = lax.rem(me + i * stride, devices)
            copy_out(
                back.at[o, target], block.at[pl.ds((me * own + o) * 16, 16)],
                (ret_send.at[o], ret_recv), target,
            ).start()
            return 0

        lax.fori_loop(1, devices, body, 0)
        block[pl.ds((me * own + o) * 16, 16), :] = back[o, me]

    for o in range(own):
        drain(field.at[o, pl.ds(0, devices - 1)], psi_recv.at[o])
        if o == 0:
            drain(pots.at[pl.ds(0, 7)], pot_recv.at[1])
        for t in range(tiles):
            work[0, t] = tile_of(field, o, t)

        def emit_one(t, value):
            work[1, t] = value

        def emit_two(t, value):
            work[2, t] = 2.0 * value - work[0, t]

        def emit_three(t, value):
            value = 2.0 * value - work[1, t]
            for b in range(nx):
                back[o, b * ny + t // 2, 8 * (t % 2) : 8 * (t % 2) + 8, :] = value[8 * b : 8 * b + 8]

        apply(0, emit_one)
        apply(1, emit_two)
        apply(2, emit_three)
        send_back(o)

    drain(block.at[pl.ds(0, (devices - 1) * own * 16)], ret_recv)

    for j in range(16):
        matrix[:, j * LANES : (j + 1) * LANES] = block[pl.ds(j, orbits, stride=16), :]

    ncount = float(rows * tiles * LANES)
    upper = orbits // 2

    def total_gram(local):
        low_lane = lax.broadcasted_iota(jnp.int32, (upper, 2 * orbits), 1) < orbits
        for i in range(2):
            sum_a[my_plane, i] = jnp.where(low_lane, local[i][:upper], local[i][upper:])
        for step in range(1, planes):
            here = sum_a.at[my_plane]
            copy_out(here, here, (sum_send.at[0], sum_recv.at[0]), plane_peer(step)).start()
        drain(sum_a.at[pl.ds(0, planes - 1)], sum_recv.at[0])
        total = sum_a[0, 0], sum_a[0, 1]
        for i in range(1, planes):
            total = pair_add(total, (sum_a[i, 0], sum_a[i, 1]))
        for i in range(2):
            sum_b[my_place, i] = total[i]
        for step in range(1, 8):
            here = sum_b.at[my_place]
            copy_out(here, here, (sum_send.at[1], sum_recv.at[1]), place_peer(step)).start()
        drain(sum_b.at[pl.ds(0, 7)], sum_recv.at[1])
        total = sum_b[0, 0], sum_b[0, 1]
        for i in range(1, 8):
            total = pair_add(total, (sum_b[i, 0], sum_b[i, 1]))
        total = settle(total)
        return [
            jnp.concatenate([part, pltpu.roll(part, orbits, 1)], axis=0) * (1.0 / ncount) for part in total
        ]

    def tiles_of(array):
        return [array[8 * i : 8 * i + 8] for i in range(orbits // 8)]

    parts = slices((matrix[...], None), 4)
    gram = total_gram(exact_products(parts, parts, 8 * LANES))
    inverse = inverse_factor(tiles_of(gram[0]))
    matrix[...] = dot_nn(inverse, matrix[...])
    store = pltpu.make_async_copy(matrix, first_ref, load_sem.at[0])
    store.start()
    inverse_parts = slices((inverse, None), 6)
    gram_parts = slices((gram[0][:, :orbits], gram[1][:, :orbits]), 6)
    half_way = exact_products(inverse_parts, gram_parts, orbits)
    half_parts = slices((half_way[0][:, :orbits], half_way[1][:, :orbits]), 6)
    second = exact_products(half_parts, inverse_parts, orbits)
    factor_ref[...] = inverse_factor(tiles_of(second[0]))

    store.wait()
    drain(pots.at[pl.ds(0, 7)], pot_send.at[1])
    for o in range(own):
        drain(field.at[o, pl.ds(0, devices - 1)], psi_send.at[o])
        drain(back.at[o, pl.ds(0, devices - 1)], ret_send.at[o])
    drain(sum_a.at[pl.ds(0, planes - 1)], sum_send.at[0])
    drain(sum_b.at[pl.ds(0, 7)], sum_send.at[1])


def finish(factor_ref, first_ref, out_ref):
    orbits = factor_ref.shape[0]
    value = dot_nn(factor_ref[...], first_ref[...])
    flat = out_ref.reshape(orbits * 8, LANES)
    for r in range(8):
        flat[pl.ds(r, orbits, stride=8), :] = value[:, r * LANES : (r + 1) * LANES]


def transposed(nx, ny, psi, potential):
    orbits = psi.shape[0]
    devices = nx * ny
    own = orbits // devices
    f32 = jnp.float32
    tiles, rows = 2 * ny, 8 * nx
    dma = pltpu.SemaphoreType.DMA
    first, factor = pl.pallas_call(
        functools.partial(kernel, nx, ny),
        out_shape=(
            jax.ShapeDtypeStruct((orbits, 16 * LANES), f32),
            jax.ShapeDtypeStruct((orbits, orbits), f32),
        ),
        in_specs=[pl.BlockSpec(memory_space=pl.ANY)] * 2,
        out_specs=(pl.BlockSpec(memory_space=pl.ANY), pl.BlockSpec(memory_space=pltpu.VMEM)),
        scratch_shapes=[
            pltpu.VMEM((orbits, 16, LANES), f32),
            pltpu.VMEM((own, devices, 16, LANES), f32),
            pltpu.VMEM((8, devices // 8, 16, LANES), f32),
            pltpu.VMEM((3, tiles, rows, LANES), f32),
            pltpu.VMEM((tiles, rows, LANES), f32),
            pltpu.VMEM((tiles, rows, LANES), f32),
            pltpu.VMEM((own, devices, 16, LANES), f32),
            pltpu.VMEM((orbits * 16, LANES), f32),
            pltpu.VMEM((orbits, 16 * LANES), f32),
            pltpu.VMEM((16, LANES), f32),
            pltpu.VMEM((devices // 8, 2, orbits // 2, 2 * orbits), f32),
            pltpu.VMEM((8, 2, orbits // 2, 2 * orbits), f32),
            dma((4,)), dma((own,)), dma((own,)), dma((own,)), dma,
            dma((2,)), dma((2,)), dma((2,)), dma((2,)),
        ],
        compiler_params=pltpu.CompilerParams(
            collective_id=0, has_side_effects=True
        ),
    )(psi, potential)
    return pl.pallas_call(
        finish,
        grid=(2,),
        out_shape=jax.ShapeDtypeStruct(psi.shape, f32),
        in_specs=[
            pl.BlockSpec((orbits, orbits), lambda h: (0, 0)),
            pl.BlockSpec((orbits, 8 * LANES), lambda h: (0, h)),
        ],
        out_specs=pl.BlockSpec((orbits, 8, LANES), lambda h: (0, 0, h)),
    )(factor, first)


def solution(mesh):
    in_specs = (P(None, "gx", "gy"), P("gx", "gy"))
    out_specs = P(None, "gx", "gy")
    nx, ny = mesh.shape["gx"], mesh.shape["gy"]

    def step(psi, potential):
        orbits, rows, lanes = psi.shape
        whole_orbits = orbits % (nx * ny) == 0 and (nx * ny) % 16 == 0
        if whole_orbits and rows == 8 and lanes == 2 * LANES and orbits == 64 and ny >= 4:
            return transposed(nx, ny, psi, potential)
        return on_device(psi, potential)

    return jax.shard_map(step, mesh=mesh, in_specs=in_specs, out_specs=out_specs, check_vma=False)
```

```python
import functools
import math

import jax
import jax.numpy as jnp
from jax import lax
from jax.experimental import pallas as pl
from jax.experimental.pallas import tpu as pltpu
from jax.sharding import PartitionSpec as P

NZ = 64


COEFS = (-205.0 / 72.0, 8.0 / 5.0, -1.0 / 5.0, 8.0 / 315.0, -1.0 / 560.0)
CENTER = 6.5
HALF_WIDTH = 5.5


def padded(array, sides, width):
    for axis, dim in sides:
        size, length = (lax.axis_size(axis), array.shape[dim])
        up = [(i, (i + 1) % size) for i in range(size)]
        down = [(j, i) for i, j in up]
        last = lax.slice_in_dim(array, length - width, length, axis=dim)
        first = lax.slice_in_dim(array, 0, width, axis=dim)
        before = lax.ppermute(last, axis, up)
        after = lax.ppermute(first, axis, down)
        array = jnp.concatenate([before, array, after], axis=dim)
    return array


def along_third(field, depth_index):
    laplace = 3.0 * COEFS[0] * field
    for distance in range(1, 5):
        forward = jnp.where(
            depth_index < NZ - distance,
            jnp.roll(field, -distance, 2),
            jnp.roll(field, NZ - distance, 2),
        )
        behind = jnp.where(
            depth_index >= distance, jnp.roll(field, distance, 2), jnp.roll(field, distance - NZ, 2)
        )
        laplace = laplace + COEFS[distance] * (forward + behind)
    return laplace


def hamiltonian(field, field_pot, depth_index):
    row_count = field.shape[1]
    lane_count = field.shape[2]
    padded_x = padded(field, (("gx", 1),), 4)
    laplace = along_third(field, depth_index)
    padded_y = padded(field, (("gy", 2),), 4 * NZ)
    for distance in range(1, 5):
        laplace = laplace + COEFS[distance] * (
            padded_x[:, 4 + distance : 4 + distance + row_count]
            + padded_x[:, 4 - distance : 4 - distance + row_count]
        )
        ahead_start = (4 + distance) * NZ
        back_start = (4 - distance) * NZ
        laplace = laplace + COEFS[distance] * (
            padded_y[:, :, ahead_start : ahead_start + lane_count]
            + padded_y[:, :, back_start : back_start + lane_count]
        )
    return -0.5 * laplace + field_pot * field


def orthonormal(matrix, ncount):
    local_gram = jnp.dot(matrix, matrix.T, precision=lax.Precision.HIGHEST) / ncount
    total_gram = lax.psum(local_gram, ("gx", "gy"))
    lower_factor = jnp.linalg.cholesky(total_gram)
    return lax.linalg.triangular_solve(lower_factor, matrix, left_side=True, lower=True)


def on_device(psi, potential):
    orbit_count = psi.shape[0]
    row_count = psi.shape[1]
    lane_count = psi.shape[2]
    field_pot = potential.reshape(1, row_count, lane_count)
    depth_index = lax.broadcasted_iota(jnp.int32, (1, 1, lane_count), 2) % NZ
    level_one = (hamiltonian(psi, field_pot, depth_index) - CENTER * psi) / HALF_WIDTH
    second = (
        2.0 * (hamiltonian(level_one, field_pot, depth_index) - CENTER * level_one) / HALF_WIDTH
        - psi
    )
    filtered = (
        2.0 * (hamiltonian(second, field_pot, depth_index) - CENTER * second) / HALF_WIDTH
        - level_one
    )
    matrix = filtered.reshape(orbit_count, row_count * lane_count)
    ncount = float(row_count * lane_count * lax.axis_size("gx") * lax.axis_size("gy"))
    first_pass = orthonormal(matrix, ncount)
    final_pass = orthonormal(first_pass, ncount)
    return final_pass.reshape(orbit_count, row_count, lane_count)


MESH = pl.DeviceIdType.MESH
EXACT = lax.Precision.HIGHEST
LANES = 128


def z_matrix():
    row = lax.broadcasted_iota(jnp.int32, (LANES, LANES), 0)
    col = lax.broadcasted_iota(jnp.int32, (LANES, LANES), 1)
    same = (row // NZ) == (col // NZ)
    gap = (row - col + 2 * NZ) % NZ
    gap = jnp.minimum(gap, NZ - gap)
    matrix = jnp.zeros((LANES, LANES), jnp.float32)
    for distance in range(5):
        if distance == 0:
            value = (-1.5 * COEFS[0] - CENTER) / HALF_WIDTH
        else:
            value = -0.5 * COEFS[distance] / HALF_WIDTH
        matrix = jnp.where(same & (gap == distance), value, matrix)
    return matrix


def dot_nn(a, b):
    return lax.dot_general(a, b, (((1,), (0,)), ((), ())), precision=EXACT, preferred_element_type=jnp.float32)


def dot_nt(a, b):
    return lax.dot_general(a, b, (((1,), (1,)), ((), ())), precision=EXACT, preferred_element_type=jnp.float32)


def inverse_factor(gram):
    tiles = len(gram)
    count = 8 * tiles
    shape = (8, 2 * count)
    row_in = lax.broadcasted_iota(jnp.int32, shape, 0)
    lane = lax.broadcasted_iota(jnp.int32, shape, 1)
    blocks = []
    for i in range(tiles):
        eye = jnp.where(lane == row_in + 8 * i + count, 1.0, 0.0)
        blocks.append(jnp.where(lane < count, gram[i], eye))

    def row_of(array, j):
        return jnp.broadcast_to(array[j : j + 1, :], shape)

    out = []
    for t in range(tiles):
        cols = [[jnp.broadcast_to(blocks[i][:, 8 * t + j : 8 * t + j + 1], shape) for j in range(8)] for i in range(t, tiles)]
        diag = [[row_of(cols[0][j], a) if a >= j else None for j in range(8)] for a in range(8)]
        inverse, pivots = [], []
        factor = [[None] * 8 for _ in range(8)]
        for j in range(8):
            pivots.append(diag[j][j])
            guess = pl.reciprocal(diag[j][j], approx=True)
            guess = guess * (2.0 - diag[j][j] * guess)
            inverse.append(guess * (2.0 - diag[j][j] * guess))
            for a in range(j + 1, 8):
                factor[a][j] = diag[a][j] * inverse[j]
            for a in range(j + 1, 8):
                for b in range(j + 1, a + 1):
                    diag[a][b] = diag[a][b] - factor[a][j] * diag[b][j]
        current = blocks[t]
        finished = []
        for j in range(8):
            finished.append(row_of(current, j))
            if j < 7:
                below = jnp.zeros(shape, jnp.float32)
                for a in range(j + 1, 8):
                    below = jnp.where(row_in == a, factor[a][j], below)
                current = current - below * finished[j]
        blocks[t] = current
        for i in range(t + 1, tiles):
            col = cols[i - t]
            total = blocks[i]
            for j in range(8):
                scaled = col[j] * inverse[j]
                total = total - scaled * finished[j]
                for b in range(j + 1, 8):
                    col[b] = col[b] - scaled * diag[b][j]
            blocks[i] = total
        pivot = pivots[0]
        for j in range(1, 8):
            pivot = jnp.where(row_in == j, pivots[j], pivot)
        out.append((current / jnp.sqrt(pivot))[:, count:])
    return jnp.concatenate(out, axis=0)


def two_sum(a, b):
    total = a + b
    part = total - a
    return total, (a - (total - part)) + (b - part)


def pair_add(first, second):
    total, rest = two_sum(first[0], second[0])
    return total, rest + (first[1] + second[1])


def settle(pair):
    total = pair[0] + pair[1]
    return total, pair[1] - (total - pair[0])


def slices(pair, count):
    value, rest = pair
    size = jnp.max(jnp.abs(value), axis=1, keepdims=True) * 2.0**17
    out = []
    for p in range(count):
        if p == 3 and rest is not None:
            value = value + rest
        unit = size * 2.0 ** (-7 * p)
        term = (value + unit) - unit
        out.append(term.astype(jnp.bfloat16))
        value = value - term
    return out


def exact_products(left, right, depth):
    rows, total = left[0].shape
    stacked = jnp.concatenate(left, axis=0)
    pair = None
    for start in range(0, total, depth):
        orders = {}
        for q in range(0, len(right), 2):
            other = jnp.concatenate(right[q : q + 2], axis=0)
            product = lax.dot_general(
                stacked[:, start : start + depth], other[:, start : start + depth],
                (((1,), (1,)), ((), ())), preferred_element_type=jnp.float32,
            )
            for p in range(len(left)):
                block = product[rows * p : rows * p + rows]
                orders[p + q] = orders[p + q] + block if p + q in orders else block
        for order in sorted(orders):
            if pair is None:
                pair = orders[order], jnp.zeros_like(orders[order])
            else:
                value, rest = two_sum(pair[0], orders[order])
                pair = value, pair[1] + rest
    turned = pltpu.roll(pair[0], rows, 1), pltpu.roll(pair[1], rows, 1)
    return settle(pair_add(pair, turned))


def kernel(
    nx, ny, psi_ref, pot_ref, first_ref, factor_ref,
    send, field, pots, work, half, zpart, back, block, matrix, pot_in, sum_a, sum_b, load_sem,
    psi_send, psi_recv, ret_send, ret_recv, pot_send, pot_recv, sum_send, sum_recv,
):
    devices = nx * ny
    orbits = psi_ref.shape[0]
    own = orbits // devices
    planes = devices // 8
    me = lax.axis_index("gx") * ny + lax.axis_index("gy")
    my_plane, my_place = me // 8, me % 8

    def device(target):
        return (target // ny, target % ny)

    def place_peer(step):
        return my_plane * 8 + lax.rem(my_place + step, 8)

    def plane_peer(step):
        return lax.rem(my_plane + step, planes) * 8 + my_place

    loads = []
    for h in range(2):
        half_lanes = pl.ds(h * LANES, LANES)
        loads.append(pltpu.make_async_copy(
            psi_ref.at[:, :, half_lanes], send.at[:, pl.ds(8 * h, 8), :], load_sem.at[h]))
    for h in range(2):
        half_lanes = pl.ds(h * LANES, LANES)
        loads.append(pltpu.make_async_copy(
            pot_ref.at[:, half_lanes], pot_in.at[pl.ds(8 * h, 8), :], load_sem.at[2 + h]))
    for c in loads:
        c.start()

    barrier = pltpu.get_barrier_semaphore()

    def greet(i, _):
        pl.semaphore_signal(barrier, inc=1, device_id=device(lax.rem(me + i, devices)), device_id_type=MESH)
        return 0

    lax.fori_loop(1, devices, greet, 0)

    for c in loads[2:]:
        c.wait()
    pots[my_place, my_plane] = pot_in[...] * (1.0 / HALF_WIDTH)
    pl.semaphore_wait(barrier, devices - 1)

    def copy_out(src, dst, sems, target):
        return pltpu.make_async_remote_copy(
            src_ref=src, dst_ref=dst, send_sem=sems[0], recv_sem=sems[1],
            device_id=device(target), device_id_type=MESH,
        )

    def drain(ref, sem):
        pltpu.make_async_copy(ref, ref, sem).wait()

    for step in range(1, planes):
        here = pots.at[my_place, my_plane]
        copy_out(here, here, (pot_send.at[0], pot_recv.at[0]), plane_peer(step)).start()

    for c in loads[:2]:
        c.wait()

    stride = next(n for n in (13, 11, 7, 5, 3, 1) if math.gcd(n, devices) == 1)

    def send_psi(i, _):
        target = lax.rem(me + i * stride, devices)
        copy_out(
            send.at[pl.ds(target * own, own)], field.at[me], (psi_send, psi_recv), target
        ).start()
        return 0

    lax.fori_loop(1, devices, send_psi, 0)
    field[me] = send[pl.ds(me * own, own)]
    drain(pots.at[0, pl.ds(0, planes - 1)], pot_recv.at[0])
    drain(pots.at[0, pl.ds(0, planes - 1)], pot_send.at[0])
    for step in range(1, 8):
        here = pots.at[my_place]
        copy_out(here, here, (pot_send.at[1], pot_recv.at[1]), place_peer(step)).start()

    zmat = z_matrix()
    tiles = 2 * ny
    rows = 8 * nx
    low = lax.broadcasted_iota(jnp.int32, (rows, LANES), 1) < NZ
    weights = [-0.5 * c / HALF_WIDTH for c in COEFS]

    def tile_of(ref, o, t):
        return jnp.concatenate(
            [ref[b * ny + t // 2, o, 8 * (t % 2) : 8 * (t % 2) + 8, :] for b in range(nx)], axis=0
        )

    def pot_tile(t):
        parts = []
        for b in range(nx):
            d = b * ny + t // 2
            parts.append(pots[d % 8, d // 8, 8 * (t % 2) : 8 * (t % 2) + 8, :])
        return jnp.concatenate(parts, axis=0)

    def apply(src, emit):
        zpart[...] = dot_nn(work[src].reshape(tiles * rows, LANES), zmat).reshape(tiles, rows, LANES)
        for t in range(tiles):
            half[t] = pltpu.roll(work[src, t], NZ, 1)
        for t in range(tiles):
            v = work[src, t]
            total = zpart[t] + pot_tile(t) * v
            for d in range(1, 5):
                total = total + weights[d] * (pltpu.roll(v, d, 0) + pltpu.roll(v, rows - d, 0))
            total = total + weights[2] * (work[src, (t + 1) % tiles] + work[src, (t - 1) % tiles])
            total = total + weights[4] * (work[src, (t + 2) % tiles] + work[src, (t - 2) % tiles])
            s = [half[(t + k) % tiles] for k in range(-2, 3)]
            total = total + weights[1] * (s[2] + jnp.where(low, s[1], s[3]))
            total = total + weights[3] * jnp.where(low, s[3] + s[0], s[4] + s[1])
            emit(t, total)

    def send_back(o):
        def body(i, _):
            target = lax.rem(me + i * stride, devices)
            copy_out(
                back.at[o, target], block.at[pl.ds((me * own + o) * 16, 16)],
                (ret_send.at[o], ret_recv), target,
            ).start()
            return 0

        lax.fori_loop(1, devices, body, 0)
        block[pl.ds((me * own + o) * 16, 16), :] = back[o, me]

    for o in range(own):
        if o == 0:
            drain(field.at[pl.ds(0, devices - 1)], psi_recv)
            drain(pots.at[pl.ds(0, 7)], pot_recv.at[1])
        for t in range(tiles):
            work[0, t] = tile_of(field, o, t)

        def emit_one(t, value):
            work[1, t] = value

        def emit_two(t, value):
            work[2, t] = 2.0 * value - work[0, t]

        def emit_three(t, value):
            value = 2.0 * value - work[1, t]
            for b in range(nx):
                back[o, b * ny + t // 2, 8 * (t % 2) : 8 * (t % 2) + 8, :] = value[8 * b : 8 * b + 8]

        apply(0, emit_one)
        apply(1, emit_two)
        apply(2, emit_three)
        send_back(o)

    drain(block.at[pl.ds(0, (devices - 1) * own * 16)], ret_recv)

    for j in range(16):
        matrix[:, j * LANES : (j + 1) * LANES] = block[pl.ds(j, orbits, stride=16), :]

    ncount = float(rows * tiles * LANES)
    mid = orbits // 2
    lane = lax.broadcasted_iota(jnp.int32, (mid, 2 * orbits), 1)

    def total_gram(local):
        value, rest = local
        corner = jnp.where(lane % orbits < mid, value[:mid], pltpu.roll(rest[:mid], mid, 1))
        quarter = mid // 2
        sum_a[my_plane, :mid] = jnp.where(lane < orbits, value[mid:], rest[mid:])
        sum_a[my_plane, mid:] = jnp.where(lane[:quarter] < orbits, corner[:quarter], corner[quarter:])

        def add_up(ref, count):
            total = ref[0]
            lost = jnp.zeros_like(total)
            for i in range(1, count):
                total, part = two_sum(total, ref[i])
                lost = lost + part
            first_part = jnp.where(lane >= orbits, pltpu.roll(lost[:mid], orbits, 1), 0.0)
            second_part = jnp.where(lane[:quarter] % orbits >= mid, pltpu.roll(lost[mid:], mid, 1), 0.0)
            return total + jnp.concatenate([first_part, second_part], axis=0)

        for step in range(1, planes):
            here = sum_a.at[my_plane]
            copy_out(here, here, (sum_send.at[0], sum_recv.at[0]), plane_peer(step)).start()
        drain(sum_a.at[pl.ds(0, planes - 1)], sum_recv.at[0])
        sum_b[my_place] = add_up(sum_a, planes)
        for step in range(1, 8):
            here = sum_b.at[my_place]
            copy_out(here, here, (sum_send.at[1], sum_recv.at[1]), place_peer(step)).start()
        drain(sum_b.at[pl.ds(0, 7)], sum_recv.at[1])
        total = add_up(sum_b, 8) * (1.0 / ncount)
        corner = jnp.concatenate([total[mid:], pltpu.roll(total[mid:], orbits, 1)], axis=0)
        out = []
        for lower, diagonal in ((total[:mid], corner), (pltpu.roll(total[:mid], orbits, 1), pltpu.roll(corner, 2 * orbits - mid, 1))):
            square = jnp.concatenate([lower, jnp.zeros((2 * orbits - mid, 2 * orbits), jnp.float32)], axis=0)
            across = pltpu.roll(square.T[:mid], mid, 1)
            out.append(jnp.concatenate([jnp.where(lane < mid, diagonal, across), lower], axis=0))
        return settle(out)

    def tiles_of(array):
        return [array[8 * i : 8 * i + 8] for i in range(orbits // 8)]

    parts = slices((matrix[...], None), 4)
    gram = total_gram(exact_products(parts, parts, 8 * LANES))
    inverse = inverse_factor(tiles_of(gram[0]))
    matrix[...] = dot_nn(inverse, matrix[...])
    store = pltpu.make_async_copy(matrix, first_ref, load_sem.at[0])
    store.start()
    inverse_parts = slices((inverse, None), 6)
    gram_parts = slices((gram[0][:, :orbits], gram[1][:, :orbits]), 6)
    half_way = exact_products(inverse_parts, gram_parts, orbits)
    half_parts = slices((half_way[0][:, :orbits], half_way[1][:, :orbits]), 6)
    second = exact_products(half_parts, inverse_parts, orbits)
    factor_ref[...] = inverse_factor(tiles_of(second[0]))

    store.wait()
    drain(field.at[pl.ds(0, devices - 1)], psi_send)
    drain(pots.at[pl.ds(0, 7)], pot_send.at[1])
    for o in range(own):
        drain(back.at[o, pl.ds(0, devices - 1)], ret_send.at[o])
    drain(sum_a.at[pl.ds(0, planes - 1)], sum_send.at[0])
    drain(sum_b.at[pl.ds(0, 7)], sum_send.at[1])


def finish(factor_ref, first_ref, out_ref):
    orbits = factor_ref.shape[0]
    value = dot_nn(factor_ref[...], first_ref[...])
    flat = out_ref.reshape(orbits * 8, LANES)
    for r in range(8):
        flat[pl.ds(r, orbits, stride=8), :] = value[:, r * LANES : (r + 1) * LANES]


def transposed(nx, ny, psi, potential):
    orbits = psi.shape[0]
    devices = nx * ny
    own = orbits // devices
    f32 = jnp.float32
    tiles, rows = 2 * ny, 8 * nx
    dma = pltpu.SemaphoreType.DMA
    first, factor = pl.pallas_call(
        functools.partial(kernel, nx, ny),
        out_shape=(
            jax.ShapeDtypeStruct((orbits, 16 * LANES), f32),
            jax.ShapeDtypeStruct((orbits, orbits), f32),
        ),
        in_specs=[pl.BlockSpec(memory_space=pl.ANY)] * 2,
        out_specs=(pl.BlockSpec(memory_space=pl.ANY), pl.BlockSpec(memory_space=pltpu.VMEM)),
        scratch_shapes=[
            pltpu.VMEM((orbits, 16, LANES), f32),
            pltpu.VMEM((devices, own, 16, LANES), f32),
            pltpu.VMEM((8, devices // 8, 16, LANES), f32),
            pltpu.VMEM((3, tiles, rows, LANES), f32),
            pltpu.VMEM((tiles, rows, LANES), f32),
            pltpu.VMEM((tiles, rows, LANES), f32),
            pltpu.VMEM((own, devices, 16, LANES), f32),
            pltpu.VMEM((orbits * 16, LANES), f32),
            pltpu.VMEM((orbits, 16 * LANES), f32),
            pltpu.VMEM((16, LANES), f32),
            pltpu.VMEM((devices // 8, 3 * orbits // 4, 2 * orbits), f32),
            pltpu.VMEM((8, 3 * orbits // 4, 2 * orbits), f32),
            dma((4,)), dma, dma, dma((own,)), dma,
            dma((2,)), dma((2,)), dma((2,)), dma((2,)),
        ],
        compiler_params=pltpu.CompilerParams(
            collective_id=0, has_side_effects=True
        ),
    )(psi, potential)
    return pl.pallas_call(
        finish,
        grid=(2,),
        out_shape=jax.ShapeDtypeStruct(psi.shape, f32),
        in_specs=[
            pl.BlockSpec((orbits, orbits), lambda h: (0, 0)),
            pl.BlockSpec((orbits, 8 * LANES), lambda h: (0, h)),
        ],
        out_specs=pl.BlockSpec((orbits, 8, LANES), lambda h: (0, 0, h)),
    )(factor, first)


def solution(mesh):
    in_specs = (P(None, "gx", "gy"), P("gx", "gy"))
    out_specs = P(None, "gx", "gy")
    nx, ny = mesh.shape["gx"], mesh.shape["gy"]

    def step(psi, potential):
        orbits, rows, lanes = psi.shape
        whole_orbits = orbits % (nx * ny) == 0 and (nx * ny) % 16 == 0
        if whole_orbits and rows == 8 and lanes == 2 * LANES and orbits == 64 and ny >= 4:
            return transposed(nx, ny, psi, potential)
        return on_device(psi, potential)

    return jax.shard_map(step, mesh=mesh, in_specs=in_specs, out_specs=out_specs, check_vma=False)
```
